128 devices in a mesh: var: 8 (over y, core), tm: 16 (over x, z).
Axes of the slice: x: 4, y: 4, z: 4, core: 2. Of those that a mesh axis runs over, the one named last changes fastest.
Arguments:
- tokens: bfloat16 [1024, 32, 1024], P('var', 'tm'), may hold values from -6 to 6
- gain: float32 [1024], replicated, may hold values from 0.25 to 1.75
- w_query: bfloat16 [1024, 1024], replicated, may hold values from -0.5 to 0.5
- w_key: bfloat16 [1024, 1024], replicated, may hold values from -0.21875 to 0.21875
- w_value: bfloat16 [1024, 1024], replicated, may hold values from -0.1875 to 0.1875
- w_out: bfloat16 [1024, 1024], replicated, may hold values from -0.1875 to 0.1875
- adjacency: int32 [8, 8], replicated, may hold values from 0 to 1, as said below
Outputs:
- mixed: bfloat16 [1024, 32, 1024], P('var', 'tm')
The draws below stay inside these ranges and needn't reach their ends.
Inputs may be any that keep to these rules, and one draw needn't show every extreme that they name: `adjacency`: each row has a one on the diagonal and at most one other one; in every draw some row has two ones.
All inputs are finite; a program needn't handle non-finite values.
Results may differ from the reference program's by a relative error of at most 0.04.
Values may be sent and summed in bfloat16 or wider, within the bound.
No kernel may reach another device: no remote copies, remote signals or barrier semaphores. Data moves between devices by JAX's collectives and lax.ppermute only.
A program may use at most 192 MiB of HBM per device.

```python
import jax
import jax.numpy as jnp
from jax import lax

D = 1024
HEADS = 16
HEAD = 64
VAR_DEV = 128
NB = 8
VARS = 1024
PATCHES = 32


def draw_tokens(key, part):
    key = jax.random.fold_in(key, 5)
    return jnp.clip(jax.random.normal(key, (VARS, PATCHES, D), jnp.float32), -6.0, 6.0).astype(jnp.bfloat16)


def draw_w_query(key, part):
    key = jax.random.fold_in(key, 11)
    spread = 2.5 / D ** 0.5
    return (jnp.clip(jax.random.normal(key, (D, D), jnp.float32), -6.0, 6.0) * spread).astype(jnp.bfloat16)


def draw_w_key(key, part):
    key = jax.random.fold_in(key, 13)
    spread = 1.0 / D ** 0.5
    return (jnp.clip(jax.random.normal(key, (D, D), jnp.float32), -6.0, 6.0) * spread).astype(jnp.bfloat16)


def draw_adjacency(key, part):
    key = jax.random.fold_in(key, 7)
    first, second, third = jax.random.split(key, 3)
    offsets = jax.random.randint(first, (NB,), 1, NB)
    flags = jax.random.randint(second, (NB,), 0, 2)
    chosen = jax.random.randint(third, (), 0, NB)
    rows = jnp.arange(NB, dtype=jnp.int32)
    flags = jnp.where(rows == chosen, 1, flags)
    other = (rows + offsets) % NB
    diagonal = (rows[:, None] == rows[None, :]).astype(jnp.int32)
    extra = flags[:, None] * (rows[None, :] == other[:, None]).astype(jnp.int32)
    return (diagonal + extra).astype(jnp.int32)


def bell_draw(own_key, dims, scale, bound, held_as=jnp.bfloat16):
    entries = scale * jax.random.normal(own_key, dims, jnp.float32)
    return jnp.clip(entries, min=-bound, max=bound).astype(held_as)


def setup_inputs(seed: int = 0) -> dict:
    streams_of = jax.random.split(jax.random.key(seed), 8)
    return {
        "tokens": draw_tokens(jax.random.fold_in(streams_of[7], 71), 0),
        "gain": jnp.clip(1.0 + 0.15 * jax.random.normal(streams_of[1], (D,), jnp.float32), 0.25, 1.75),
        "w_query": draw_w_query(jax.random.fold_in(streams_of[7], 71), 0),
        "w_key": draw_w_key(jax.random.fold_in(streams_of[7], 71), 0),
        "w_value": bell_draw(streams_of[4], (D, D), D ** -0.5, 0.1875),
        "w_out": bell_draw(streams_of[5], (D, D), D ** -0.5, 0.1875),
        "adjacency": draw_adjacency(jax.random.fold_in(streams_of[7], 71), 0),
    }


def reference(tokens, gain, w_query, w_key, w_value, w_out, adjacency):
    x = tokens.astype(jnp.float32)
    meansq = lax.optimization_barrier(jnp.mean(x * x, axis=-1, keepdims=True))
    normed = (x * lax.rsqrt(meansq + 1e-06) * gain).astype(jnp.bfloat16)
    flat = normed.reshape(-1, D)
    length = VAR_DEV * PATCHES
    query = jnp.dot(flat, w_query, preferred_element_type=jnp.float32).astype(jnp.bfloat16).reshape(NB, length, HEADS, HEAD)
    key = jnp.dot(flat, w_key, preferred_element_type=jnp.float32).astype(jnp.bfloat16).reshape(NB, length, HEADS, HEAD)
    value = jnp.dot(flat, w_value, preferred_element_type=jnp.float32).astype(jnp.bfloat16).reshape(NB, length, HEADS, HEAD)
    steps = jnp.arange(length, dtype=jnp.int32) % PATCHES
    blocks = jnp.arange(NB, dtype=jnp.int32)
    scale = 1.0 / HEAD ** 0.5

    def one(index):
        block = (index // HEADS).astype(jnp.int32)
        head = (index % HEADS).astype(jnp.int32)
        row = adjacency[block]
        others = row * (blocks != block).astype(jnp.int32)
        has_other = jnp.sum(others)
        other = (jnp.sum(others * blocks) + (1 - has_other) * block).astype(jnp.int32)
        q_head = query[block, :, head, :]
        k_head = jnp.concatenate([key[block, :, head, :], key[other, :, head, :]], axis=0)
        v_head = jnp.concatenate([value[block, :, head, :], value[other, :, head, :]], axis=0)
        key_steps = jnp.concatenate([steps, steps])
        key_valid = jnp.concatenate([jnp.ones((length,), bool), jnp.full((length,), has_other > 0)])
        allowed = (key_steps[None, :] <= steps[:, None]) & key_valid[None, :]
        score = jnp.dot(q_head, k_head.T, preferred_element_type=jnp.float32) * scale
        score = jnp.where(allowed, score, jnp.float32(-1e+30))
        top = lax.optimization_barrier(jnp.max(score, axis=-1, keepdims=True))
        expo = jnp.where(allowed, jnp.exp(score - top), jnp.float32(0.0))
        total = lax.optimization_barrier(jnp.sum(expo, axis=-1, keepdims=True))
        summed = jnp.dot(expo.astype(jnp.bfloat16), v_head, preferred_element_type=jnp.float32)
        return (summed / total).astype(jnp.bfloat16)
    heads_out = lax.map(one, jnp.arange(NB * HEADS, dtype=jnp.int32))
    attended = heads_out.reshape(NB, HEADS, length, HEAD).transpose(0, 2, 1, 3).reshape(-1, D)
    mixed = jnp.dot(attended, w_out, preferred_element_type=jnp.float32).astype(jnp.bfloat16)
    return mixed.reshape(VARS, PATCHES, D)
```

```python
import functools
import math

import jax
import jax.numpy as jnp
from jax import lax
from jax.experimental import pallas as pl
from jax.experimental.pallas import tpu as pltpu
from jax.sharding import PartitionSpec as P

HEADS = 16
HEAD = 64
LANES = 2 * HEAD
COLS = 512
CHUNK = 1024
TILE = 512
LOW = -1e30
SAFE = 80.0


def exchange(x):
    return lax.all_to_all(x, "tm", split_axis=0, concat_axis=0, tiled=True)


def low_lanes(shape):
    return lax.broadcasted_iota(jnp.int32, shape, len(shape) - 1) < HEAD


def swap(x):
    return pltpu.roll(x, HEAD, x.ndim - 1)


def normed_rows(x_ref, gain_ref):
    x = x_ref[...].astype(jnp.float32)
    x = jnp.concatenate([x[:, step] for step in range(x.shape[1])], axis=0)
    meansq = jnp.mean(x * x, axis=-1, keepdims=True)
    return (x * lax.rsqrt(meansq + 1e-06) * gain_ref[...]).astype(jnp.bfloat16)


def project_kernel(with_query, *refs):
    x_ref, gain_ref, wk_ref, wv_ref = refs[:4]
    out_ref, normed_ref = refs[-2:]
    step = pl.program_id(0)

    @pl.when(step == 0)
    def _():
        normed_ref[...] = normed_rows(x_ref, gain_ref)

    normed = normed_ref[...]
    rows = normed.shape[0]
    half = rows // 2
    k = jnp.dot(normed, wk_ref[...], preferred_element_type=jnp.float32)
    v = jnp.dot(normed, wv_ref[...], preferred_element_type=jnp.float32)
    if with_query:
        q = jnp.dot(normed, refs[4][...], preferred_element_type=jnp.float32)
        q = q * (math.log2(math.e) / HEAD**0.5)
    for p in range(COLS // LANES):
        cols = slice(p * LANES, (p + 1) * LANES)
        kt, vt = k[:, cols], v[:, cols]
        low = low_lanes(kt.shape)
        out_ref[2 * p, :rows] = jnp.where(low, kt, swap(vt)).astype(jnp.bfloat16)
        out_ref[2 * p + 1, :rows] = jnp.where(low, swap(kt), vt).astype(jnp.bfloat16)
        if with_query:
            top, bottom = q[:half, cols], q[half:, cols]
            low = low_lanes(top.shape)
            out_ref[2 * p, rows:] = jnp.where(low, top, swap(bottom)).astype(jnp.bfloat16)
            out_ref[2 * p + 1, rows:] = jnp.where(low, swap(top), bottom).astype(jnp.bfloat16)


def project(x, gain, weights):
    var_rows, step_rows, width = x.shape
    rows = var_rows * step_rows
    with_query = len(weights) == 3
    out_rows = rows + rows // 2 if with_query else rows
    flops = 2 * rows * width * width * len(weights)
    return pl.pallas_call(
        functools.partial(project_kernel, with_query),
        grid=(width // COLS,),
        in_specs=[
            pl.BlockSpec(x.shape, lambda j: (0, 0, 0)),
            pl.BlockSpec((1, width), lambda j: (0, 0)),
        ]
        + [pl.BlockSpec((width, COLS), lambda j: (0, j))] * len(weights),
        out_specs=pl.BlockSpec((COLS // HEAD, out_rows, LANES), lambda j: (j, 0, 0)),
        out_shape=jax.ShapeDtypeStruct((HEADS, out_rows, LANES), jnp.bfloat16),
        scratch_shapes=[pltpu.VMEM((rows, width), jnp.bfloat16)],
        compiler_params=pltpu.CompilerParams(vmem_limit_bytes=(56 if with_query else 20) << 20),
        cost_estimate=pl.CostEstimate(
            flops=flops, bytes_accessed=2 * width * width * len(weights) + 4 * rows * width,
            transcendentals=0,
        ),
        name="project_own" if with_query else "project_other",
    )(x, gain, *weights)


def attend_kernel(final, *refs):
    q_ref, *refs = refs
    kv_ref = q_ref
    if final:
        kv_ref, state_in, longest_in, out_ref, acc, *refs = refs
    else:
        acc, longest_out, *refs = refs
    top, query, key, value, p0, p1, query_len, key_len = refs
    rows = q_ref.shape[1] * 2 // 3
    half = rows // 2
    per = TILE // rows
    tiles = HEADS // per
    lane_of = lambda axis: lax.broadcasted_iota(jnp.int32, (LANES, LANES), axis) // HEAD
    same_half = (lane_of(0) == lane_of(1)).astype(jnp.bfloat16)
    key_half = (lane_of(0) == 0).astype(jnp.bfloat16)

    def lengths(x, ones):
        return jnp.dot((x * x).astype(jnp.bfloat16), ones, preferred_element_type=jnp.float32)

    def at(tile, count=1):
        return pl.ds(pl.multiple_of(tile * TILE, TILE), count * TILE)

    def prepare(t, carry):
        block = pl.ds(pl.multiple_of(t * rows, rows), rows)
        x = q_ref[t, rows:].astype(jnp.float32)
        if not final:
            query_len[...] = jnp.maximum(query_len[...], lengths(x, same_half))
        low = low_lanes(x.shape)
        lane = lax.broadcasted_iota(jnp.int32, x.shape, 1) - HEAD
        for part, y in enumerate((x, swap(x))):
            step = 2 * (t % per) + part
            later = jnp.where((lane > step) & (lane < 2 * per), LOW, jnp.float32(0.0))
            first = jnp.where(t // per % 2 == 0, later, 0.0)
            to = pl.ds(pl.multiple_of(t * rows + part * half, half), half)
            for n, mask in enumerate((0.0, first, later)):
                query[n, to] = jnp.where(low, y, mask).astype(jnp.bfloat16)
        kv = kv_ref[t, :rows].astype(jnp.float32)
        key_len[...] = jnp.maximum(key_len[...], lengths(kv, key_half))
        low = low_lanes(kv.shape)
        lane = lax.broadcasted_iota(jnp.int32, kv.shape, 1) - HEAD
        step = 2 * (t % per) + lax.broadcasted_iota(jnp.int32, kv.shape, 0) // half
        is_step = jnp.where(lane == step, jnp.float32(1.0), jnp.float32(0.0))
        key[block] = jnp.where(low, kv, is_step).astype(jnp.bfloat16)
        value[block] = jnp.where(low, 1.0, kv).astype(jnp.bfloat16)
        acc[block] = state_in[block] if final else jnp.zeros((rows, LANES), jnp.float32)
        return carry

    query_len[...] = jnp.zeros_like(query_len)
    key_len[...] = jnp.zeros_like(key_len)
    lax.fori_loop(0, HEADS, prepare, 0, unroll=2)
    longest = longest_in[0] if final else jnp.max(query_len[...])
    fits = longest * jnp.max(key_len[...]) <= SAFE * SAFE
    if final:
        own_fits = longest >= 0.0
        fits = fits & own_fits
    else:
        longest_out[0] = jnp.where(fits, longest, -1.0)

    def scores(q, j):
        return lax.dot_general(
            q, key[at(j)], (((1,), (1,)), ((), ())), preferred_element_type=jnp.float32
        )

    def weighted(p, j):
        return jnp.dot(p, value[at(j)], preferred_element_type=jnp.float32)

    @pl.when(fits)
    def _():
        def weights(p, j, first):
            diagonal = (j == first).astype(jnp.int32)
            p[...] = jnp.exp2(scores(query[diagonal, at(first, 2)], j)).astype(jnp.bfloat16)

        def gather(p, j, first):
            acc[at(first, 2)] += weighted(p[...], j)

        def late_weights(p, j):
            p[:TILE] = jnp.exp2(scores(query[2, at(j)], j)).astype(jnp.bfloat16)

        def late_gather(p, j):
            acc[at(j)] += weighted(p[:TILE], j)

        def chunk(a, carry):
            first = 2 * a

            def turn(n, carry):
                j = 2 * n
                weights(p1, j + 1, first)
                gather(p0, j, first)
                weights(p0, j + 2, first)
                gather(p1, j + 1, first)
                return carry

            lax.fori_loop(0, a, turn, 0)
            late_weights(p1, first + 1)
            gather(p0, first, first)
            weights(p0, jnp.int32(0), jnp.minimum(first + 2, tiles - 2))
            late_gather(p1, first + 1)
            return carry

        weights(p0, jnp.int32(0), jnp.int32(0))
        lax.fori_loop(0, tiles // 2, chunk, 0)

    @pl.when(jnp.logical_not(fits))
    def _():
        lane = lax.broadcasted_iota(jnp.int32, (TILE, LANES), 1)

        def spread(x, n):
            return jnp.max(jnp.where(lane == n, x, -jnp.inf), axis=-1, keepdims=True)

        def row_block(i, carry):
            to = at(i)
            if final:
                x = acc[to]
                top[...] = jnp.where(own_fits, 0.0, spread(x, HEAD // 2)) + jnp.zeros_like(x)
                acc[to] = jnp.where(lane < HEAD, spread(x, 0), x)
            else:
                top[...] = jnp.full_like(top, LOW)

            def key_block(j, carry):
                s = scores(query[2 * (i == j).astype(jnp.int32), to], j)
                old = top[...]
                new = jnp.maximum(old, jnp.max(s, axis=-1, keepdims=True))
                p = jnp.exp2(s - jnp.concatenate([new] * (TILE // LANES), axis=1))
                acc[to] = acc[to] * jnp.exp2(old - new) + weighted(p.astype(jnp.bfloat16), j)
                top[...] = new
                return carry

            lax.fori_loop(0, i + 1, key_block, 0)
            if not final:
                x = acc[to]
                acc[to] = jnp.where((lane >= HEAD // 2) & (lane < HEAD), top[...], x)
            return carry

        lax.fori_loop(0, tiles, row_block, 0)

    if final:

        def finish(t, carry):
            base = pl.multiple_of(t * rows, rows)
            x = acc[pl.ds(base, half)]
            y = acc[pl.ds(base + half, half)]
            low = low_lanes(x.shape)
            num = jnp.where(low, swap(x), y)
            den = jnp.where(low, x, swap(y))
            out_ref[t] = (num / den).astype(jnp.bfloat16)
            return carry

        lax.fori_loop(0, HEADS, finish, 0, unroll=2)


def attend(*operands):
    rows = operands[0].shape[1] * 2 // 3
    final = len(operands) > 1
    total = HEADS * rows
    whole = pl.BlockSpec(memory_space=pltpu.VMEM)
    scalar = pl.BlockSpec(memory_space=pltpu.SMEM)
    bf16_rows = pltpu.VMEM((total, LANES), jnp.bfloat16)
    f32_rows = pltpu.VMEM((total, LANES), jnp.float32)
    scratch = [f32_rows] * final + [
        pltpu.VMEM((TILE, LANES), jnp.float32),
        pltpu.VMEM((3, total, LANES), jnp.bfloat16),
        bf16_rows,
        bf16_rows,
        pltpu.VMEM((CHUNK, TILE), jnp.bfloat16),
        pltpu.VMEM((CHUNK, TILE), jnp.bfloat16),
        pltpu.VMEM((rows // 2, LANES), jnp.float32),
        pltpu.VMEM((rows, LANES), jnp.float32),
    ]
    if final:
        out = jax.ShapeDtypeStruct((HEADS, rows // 2, LANES), jnp.bfloat16)
    else:
        out = [
            jax.ShapeDtypeStruct((total, LANES), jnp.float32),
            jax.ShapeDtypeStruct((1,), jnp.float32),
        ]
    pairs = total * total // 2
    return pl.pallas_call(
        functools.partial(attend_kernel, final),
        in_specs=[whole, whole, whole, scalar] if final else [whole],
        out_specs=whole if final else [whole, scalar],
        out_shape=out,
        scratch_shapes=scratch,
        compiler_params=pltpu.CompilerParams(vmem_limit_bytes=20 << 20),
        cost_estimate=pl.CostEstimate(
            flops=16 * pairs * LANES, bytes_accessed=8 << 20, transcendentals=pairs
        ),
        name="attend_other" if final else "attend_own",
    )(*operands)


def out_kernel(a_ref, w_ref, o_ref, flat):
    half = a_ref.shape[1]

    for p in range(HEADS // 2):
        a = a_ref[2 * p].astype(jnp.float32)
        b = a_ref[2 * p + 1].astype(jnp.float32)
        low = low_lanes(a.shape)
        cols = slice(p * LANES, (p + 1) * LANES)
        flat[:half, cols] = jnp.where(low, a, swap(b)).astype(jnp.bfloat16)
        flat[half:, cols] = jnp.where(low, swap(a), b).astype(jnp.bfloat16)
    for c in range(0, w_ref.shape[1], COLS):
        mixed = jnp.dot(flat[...], w_ref[:, c : c + COLS], preferred_element_type=jnp.float32)
        mixed = [mixed[step * half : (step + 1) * half] for step in range(2)]
        o_ref[:, :, c : c + COLS] = jnp.stack(mixed, axis=1).astype(jnp.bfloat16)


def project_out(att, w_out):
    half = att.shape[1]
    width = w_out.shape[0]
    rows = 2 * half
    return pl.pallas_call(
        out_kernel,
        in_specs=[pl.BlockSpec(memory_space=pltpu.VMEM)] * 2,
        out_specs=pl.BlockSpec(memory_space=pltpu.VMEM),
        out_shape=jax.ShapeDtypeStruct((half, 2, width), jnp.bfloat16),
        scratch_shapes=[pltpu.VMEM((rows, width), jnp.bfloat16)],
        compiler_params=pltpu.CompilerParams(vmem_limit_bytes=24 << 20),
        cost_estimate=pl.CostEstimate(
            flops=2 * rows * width * width, bytes_accessed=2 * width * width, transcendentals=0
        ),
        name="project_out",
    )(att, w_out)


def block_for(adjacency, mine):
    blocks = jnp.arange(adjacency.shape[0], dtype=jnp.int32)
    row = lax.dynamic_index_in_dim(adjacency, mine, 0, keepdims=False)
    others = row * (blocks != mine).astype(jnp.int32)
    return jnp.sum(others * blocks) + (1 - jnp.sum(others)) * mine


def choose(index, options):
    return functools.reduce(
        lambda rest, at: jnp.where(index == at, options[at], rest),
        range(len(options) - 1),
        options[-1],
    )


def same_core(x):
    count = lax.axis_size("var")
    held = []
    for offset in range(1, count // 2):
        pairs = [(v, (v + 2 * offset) % count) for v in range(count)]
        held.append(lax.ppermute(x, "var", pairs))
    return held


def pick_other(held, adjacency):
    count = lax.axis_size("var")
    chips = count // 2
    mine = lax.axis_index("var")
    want = block_for(adjacency, mine)
    partner_want = block_for(adjacency, mine ^ 1)
    away = lambda block: (mine // 2 - block // 2 + chips) % chips
    to_send = choose(away(partner_want), held)
    got = lax.ppermute(to_send, "var", [(v, v ^ 1) for v in range(count)])
    slot = jnp.where(want % 2 == mine % 2, away(want), chips)
    return choose(slot, held + [got])


def local(tokens, gain, w_query, w_key, w_value, w_out, adjacency):
    gain = gain.reshape(1, -1)
    held = same_core(tokens)
    packed = project(tokens, gain, (w_key, w_value, w_query))
    *held, _ = lax.optimization_barrier((*held, packed))
    x_other = pick_other([tokens, *held], adjacency)
    kv_other = project(x_other, gain, (w_key, w_value))
    packed, _ = lax.optimization_barrier((exchange(packed), kv_other))
    kv_other = exchange(kv_other)
    att = exchange(attend(packed, kv_other, *attend(packed)))
    return project_out(att, w_out)


def solution(mesh):
    in_specs = (P("var", "tm", None), P(), P(), P(), P(), P(), P())
    out_specs = P("var", "tm", None)
    return jax.shard_map(local, mesh=mesh, in_specs=in_specs, out_specs=out_specs, check_vma=False)
```

```python
import functools
import math

import jax
import jax.numpy as jnp
from jax import lax
from jax.experimental import pallas as pl
from jax.experimental.pallas import tpu as pltpu
from jax.sharding import PartitionSpec as P

HEADS = 16
HEAD = 64
LANES = 2 * HEAD
COLS = 512
CHUNK = 1024
TILE = 512
LOW = -1e30
SAFE = 80.0


def exchange(x):
    return lax.all_to_all(x, "tm", split_axis=0, concat_axis=0, tiled=True)


def low_lanes(shape):
    return lax.broadcasted_iota(jnp.int32, shape, len(shape) - 1) < HEAD


def swap(x):
    return pltpu.roll(x, HEAD, x.ndim - 1)


def normed_rows(x_ref, gain_ref):
    x = x_ref[...].astype(jnp.float32)
    x = jnp.concatenate([x[:, step] for step in range(x.shape[1])], axis=0)
    meansq = jnp.mean(x * x, axis=-1, keepdims=True)
    return (x * lax.rsqrt(meansq + 1e-06) * gain_ref[...]).astype(jnp.bfloat16)


def project_kernel(with_query, *refs):
    x_ref, gain_ref, wk_ref, wv_ref = refs[:4]
    out_ref, normed_ref = refs[-2:]
    step = pl.program_id(0)

    @pl.when(step == 0)
    def _():
        normed_ref[...] = normed_rows(x_ref, gain_ref)

    normed = normed_ref[...]
    rows = normed.shape[0]
    half = rows // 2
    k = jnp.dot(normed, wk_ref[...], preferred_element_type=jnp.float32)
    v = jnp.dot(normed, wv_ref[...], preferred_element_type=jnp.float32)
    if with_query:
        q = jnp.dot(normed, refs[4][...], preferred_element_type=jnp.float32)
        q = q * (math.log2(math.e) / HEAD**0.5)
    for p in range(COLS // LANES):
        cols = slice(p * LANES, (p + 1) * LANES)
        kt, vt = k[:, cols], v[:, cols]
        low = low_lanes(kt.shape)
        out_ref[2 * p, :rows] = jnp.where(low, kt, swap(vt)).astype(jnp.bfloat16)
        out_ref[2 * p + 1, :rows] = jnp.where(low, swap(kt), vt).astype(jnp.bfloat16)
        if with_query:
            top, bottom = q[:half, cols], q[half:, cols]
            low = low_lanes(top.shape)
            out_ref[2 * p, rows:] = jnp.where(low, top, swap(bottom)).astype(jnp.bfloat16)
            out_ref[2 * p + 1, rows:] = jnp.where(low, swap(top), bottom).astype(jnp.bfloat16)


def project(x, gain, weights):
    var_rows, step_rows, width = x.shape
    rows = var_rows * step_rows
    with_query = len(weights) == 3
    out_rows = rows + rows // 2 if with_query else rows
    flops = 2 * rows * width * width * len(weights)
    return pl.pallas_call(
        functools.partial(project_kernel, with_query),
        grid=(width // COLS,),
        in_specs=[
            pl.BlockSpec(x.shape, lambda j: (0, 0, 0)),
            pl.BlockSpec((1, width), lambda j: (0, 0)),
        ]
        + [pl.BlockSpec((width, COLS), lambda j: (0, j))] * len(weights),
        out_specs=pl.BlockSpec((COLS // HEAD, out_rows, LANES), lambda j: (j, 0, 0)),
        out_shape=jax.ShapeDtypeStruct((HEADS, out_rows, LANES), jnp.bfloat16),
        scratch_shapes=[pltpu.VMEM((rows, width), jnp.bfloat16)],
        compiler_params=pltpu.CompilerParams(vmem_limit_bytes=(52 if with_query else 20) << 20),
        cost_estimate=pl.CostEstimate(
            flops=flops, bytes_accessed=2 * width * width * len(weights) + 4 * rows * width,
            transcendentals=0,
        ),
        name="project_own" if with_query else "project_other",
    )(x, gain, *weights)


def attend_kernel(final, *refs):
    q_ref, *refs = refs
    kv_ref = q_ref
    if final:
        kv_ref, state_in, longest_in, out_ref, acc, *refs = refs
    else:
        acc, longest_out, *refs = refs
    top, query, key, value, p0, p1, query_len, key_len = refs
    rows = q_ref.shape[1] * 2 // 3
    half = rows // 2
    per = TILE // rows
    tiles = HEADS // per
    lane_of = lambda axis: lax.broadcasted_iota(jnp.int32, (LANES, LANES), axis) // HEAD
    same_half = (lane_of(0) == lane_of(1)).astype(jnp.bfloat16)
    key_half = (lane_of(0) == 0).astype(jnp.bfloat16)

    def lengths(x, ones):
        return jnp.dot((x * x).astype(jnp.bfloat16), ones, preferred_element_type=jnp.float32)

    def at(tile, count=1):
        return pl.ds(pl.multiple_of(tile * TILE, TILE), count * TILE)

    def prepare(t, carry):
        block = pl.ds(pl.multiple_of(t * rows, rows), rows)
        x = q_ref[t, rows:].astype(jnp.float32)
        if not final:
            query_len[...] = jnp.maximum(query_len[...], lengths(x, same_half))
        low = low_lanes(x.shape)
        lane = lax.broadcasted_iota(jnp.int32, x.shape, 1) - HEAD
        for part, y in enumerate((x, swap(x))):
            step = 2 * (t % per) + part
            later = jnp.where((lane > step) & (lane < 2 * per), LOW, jnp.float32(0.0))
            first = jnp.where(t // per % 2 == 0, later, 0.0)
            to = pl.ds(pl.multiple_of(t * rows + part * half, half), half)
            for n, mask in enumerate((0.0, first, later)):
                query[n, to] = jnp.where(low, y, mask).astype(jnp.bfloat16)
        kv = kv_ref[t, :rows].astype(jnp.float32)
        key_len[...] = jnp.maximum(key_len[...], lengths(kv, key_half))
        low = low_lanes(kv.shape)
        lane = lax.broadcasted_iota(jnp.int32, kv.shape, 1) - HEAD
        step = 2 * (t % per) + lax.broadcasted_iota(jnp.int32, kv.shape, 0) // half
        is_step = jnp.where(lane == step, jnp.float32(1.0), jnp.float32(0.0))
        key[block] = jnp.where(low, kv, is_step).astype(jnp.bfloat16)
        value[block] = jnp.where(low, 1.0, kv).astype(jnp.bfloat16)
        acc[block] = state_in[block] if final else jnp.zeros((rows, LANES), jnp.float32)
        return carry

    query_len[...] = jnp.zeros_like(query_len)
    key_len[...] = jnp.zeros_like(key_len)
    lax.fori_loop(0, HEADS, prepare, 0, unroll=2)
    longest = longest_in[0] if final else jnp.max(query_len[...])
    fits = longest * jnp.max(key_len[...]) <= SAFE * SAFE
    if final:
        own_fits = longest >= 0.0
        fits = fits & own_fits
    else:
        longest_out[0] = jnp.where(fits, longest, -1.0)

    def scores(q, j):
        return lax.dot_general(
            q, key[at(j)], (((1,), (1,)), ((), ())), preferred_element_type=jnp.float32
        )

    def weighted(p, j):
        return jnp.dot(p, value[at(j)], preferred_element_type=jnp.float32)

    @pl.when(fits)
    def _():
        def weights(p, j, first):
            diagonal = (j == first).astype(jnp.int32)
            p[...] = jnp.exp2(scores(query[diagonal, at(first, 2)], j)).astype(jnp.bfloat16)

        def gather(p, j, first):
            acc[at(first, 2)] += weighted(p[...], j)

        def late_weights(p, j):
            p[:TILE] = jnp.exp2(scores(query[2, at(j)], j)).astype(jnp.bfloat16)

        def late_gather(p, j):
            acc[at(j)] += weighted(p[:TILE], j)

        def chunk(a, carry):
            first = 2 * a

            def turn(n, carry):
                j = 2 * n
                weights(p1, j + 1, first)
                gather(p0, j, first)
                weights(p0, j + 2, first)
                gather(p1, j + 1, first)
                return carry

            lax.fori_loop(0, a, turn, 0)
            late_weights(p1, first + 1)
            gather(p0, first, first)
            weights(p0, jnp.int32(0), jnp.minimum(first + 2, tiles - 2))
            late_gather(p1, first + 1)
            return carry

        weights(p0, jnp.int32(0), jnp.int32(0))
        lax.fori_loop(0, tiles // 2, chunk, 0)

    @pl.when(jnp.logical_not(fits))
    def _():
        lane = lax.broadcasted_iota(jnp.int32, (TILE, LANES), 1)

        def spread(x, n):
            return jnp.max(jnp.where(lane == n, x, -jnp.inf), axis=-1, keepdims=True)

        def row_block(i, carry):
            to = at(i)
            if final:
                x = acc[to]
                top[...] = jnp.where(own_fits, 0.0, spread(x, HEAD // 2)) + jnp.zeros_like(x)
                acc[to] = jnp.where(lane < HEAD, spread(x, 0), x)
            else:
                top[...] = jnp.full_like(top, LOW)

            def key_block(j, carry):
                s = scores(query[2 * (i == j).astype(jnp.int32), to], j)
                old = top[...]
                new = jnp.maximum(old, jnp.max(s, axis=-1, keepdims=True))
                p = jnp.exp2(s - jnp.concatenate([new] * (TILE // LANES), axis=1))
                acc[to] = acc[to] * jnp.exp2(old - new) + weighted(p.astype(jnp.bfloat16), j)
                top[...] = new
                return carry

            lax.fori_loop(0, i + 1, key_block, 0)
            if not final:
                x = acc[to]
                acc[to] = jnp.where((lane >= HEAD // 2) & (lane < HEAD), top[...], x)
            return carry

        lax.fori_loop(0, tiles, row_block, 0)

    if final:

        def finish(t, carry):
            base = pl.multiple_of(t * rows, rows)
            x = acc[pl.ds(base, half)]
            y = acc[pl.ds(base + half, half)]
            low = low_lanes(x.shape)
            num = jnp.where(low, swap(x), y)
            den = jnp.where(low, x, swap(y))
            out_ref[t] = (num / den).astype(jnp.bfloat16)
            return carry

        lax.fori_loop(0, HEADS, finish, 0, unroll=2)


def attend(*operands):
    rows = operands[0].shape[1] * 2 // 3
    final = len(operands) > 1
    total = HEADS * rows
    whole = pl.BlockSpec(memory_space=pltpu.VMEM)
    scalar = pl.BlockSpec(memory_space=pltpu.SMEM)
    bf16_rows = pltpu.VMEM((total, LANES), jnp.bfloat16)
    f32_rows = pltpu.VMEM((total, LANES), jnp.float32)
    scratch = [f32_rows] * final + [
        pltpu.VMEM((TILE, LANES), jnp.float32),
        pltpu.VMEM((3, total, LANES), jnp.bfloat16),
        bf16_rows,
        bf16_rows,
        pltpu.VMEM((CHUNK, TILE), jnp.bfloat16),
        pltpu.VMEM((CHUNK, TILE), jnp.bfloat16),
        pltpu.VMEM((rows // 2, LANES), jnp.float32),
        pltpu.VMEM((rows, LANES), jnp.float32),
    ]
    if final:
        out = jax.ShapeDtypeStruct((HEADS, rows // 2, LANES), jnp.bfloat16)
    else:
        out = [
            jax.ShapeDtypeStruct((total, LANES), jnp.float32),
            jax.ShapeDtypeStruct((1,), jnp.float32),
        ]
    pairs = total * total // 2
    return pl.pallas_call(
        functools.partial(attend_kernel, final),
        in_specs=[whole, whole, whole, scalar] if final else [whole],
        out_specs=whole if final else [whole, scalar],
        out_shape=out,
        scratch_shapes=scratch,
        compiler_params=pltpu.CompilerParams(vmem_limit_bytes=20 << 20),
        cost_estimate=pl.CostEstimate(
            flops=16 * pairs * LANES, bytes_accessed=8 << 20, transcendentals=pairs
        ),
        name="attend_other" if final else "attend_own",
    )(*operands)


def out_kernel(a_ref, w_ref, o_ref, flat):
    half = a_ref.shape[1]

    for p in range(HEADS // 2):
        a = a_ref[2 * p].astype(jnp.float32)
        b = a_ref[2 * p + 1].astype(jnp.float32)
        low = low_lanes(a.shape)
        cols = slice(p * LANES, (p + 1) * LANES)
        flat[:half, cols] = jnp.where(low, a, swap(b)).astype(jnp.bfloat16)
        flat[half:, cols] = jnp.where(low, swap(a), b).astype(jnp.bfloat16)
    for c in range(0, w_ref.shape[1], COLS):
        mixed = jnp.dot(flat[...], w_ref[:, c : c + COLS], preferred_element_type=jnp.float32)
        mixed = [mixed[step * half : (step + 1) * half] for step in range(2)]
        o_ref[:, :, c : c + COLS] = jnp.stack(mixed, axis=1).astype(jnp.bfloat16)


def project_out(att, w_out):
    half = att.shape[1]
    width = w_out.shape[0]
    rows = 2 * half
    return pl.pallas_call(
        out_kernel,
        in_specs=[pl.BlockSpec(memory_space=pltpu.VMEM)] * 2,
        out_specs=pl.BlockSpec(memory_space=pltpu.VMEM),
        out_shape=jax.ShapeDtypeStruct((half, 2, width), jnp.bfloat16),
        scratch_shapes=[pltpu.VMEM((rows, width), jnp.bfloat16)],
        compiler_params=pltpu.CompilerParams(vmem_limit_bytes=24 << 20),
        cost_estimate=pl.CostEstimate(
            flops=2 * rows * width * width, bytes_accessed=2 * width * width, transcendentals=0
        ),
        name="project_out",
    )(att, w_out)


def block_for(adjacency, mine):
    blocks = jnp.arange(adjacency.shape[0], dtype=jnp.int32)
    row = lax.dynamic_index_in_dim(adjacency, mine, 0, keepdims=False)
    others = row * (blocks != mine).astype(jnp.int32)
    return jnp.sum(others * blocks) + (1 - jnp.sum(others)) * mine


def choose(index, options):
    return functools.reduce(
        lambda rest, at: jnp.where(index == at, options[at], rest),
        range(len(options) - 1),
        options[-1],
    )


def along_y(x, offset):
    count = lax.axis_size("var")
    pairs = [(v, (v + 2 * offset) % count) for v in range(count)]
    return lax.ppermute(x, "var", pairs)


def pick_other(held, adjacency):
    count = lax.axis_size("var")
    chips = count // 2
    mine = lax.axis_index("var")
    want = block_for(adjacency, mine)
    partner_want = block_for(adjacency, mine ^ 1)
    away = lambda block: (mine // 2 - block // 2 + chips) % chips
    to_send = choose(away(partner_want), held)
    got = lax.ppermute(to_send, "var", [(v, v ^ 1) for v in range(count)])
    slot = jnp.where(want % 2 == mine % 2, away(want), chips)
    return choose(slot, held + [got])


def local(tokens, gain, w_query, w_key, w_value, w_out, adjacency):
    gain = gain.reshape(1, -1)
    below, above = along_y(tokens, 1), along_y(tokens, -1)
    packed = project(tokens, gain, (w_key, w_value, w_query))
    below, above, _ = lax.optimization_barrier((below, above, packed))
    middle = tokens.shape[0] // 2
    across = jnp.concatenate([along_y(below[:middle], 1), along_y(above[middle:], -1)], axis=0)
    x_other = pick_other([tokens, below, across, above], adjacency)
    kv_other = project(x_other, gain, (w_key, w_value))
    packed, _ = lax.optimization_barrier((exchange(packed), kv_other))
    kv_other = exchange(kv_other)
    att = exchange(attend(packed, kv_other, *attend(packed)))
    return project_out(att, w_out)


def solution(mesh):
    in_specs = (P("var", "tm", None), P(), P(), P(), P(), P(), P())
    out_specs = P("var", "tm", None)
    return jax.shard_map(local, mesh=mesh, in_specs=in_specs, out_specs=out_specs, check_vma=False)
```

```python
import functools
import math

import jax
import jax.numpy as jnp
from jax import lax
from jax.experimental import pallas as pl
from jax.experimental.pallas import tpu as pltpu
from jax.sharding import PartitionSpec as P

HEADS = 16
HEAD = 64
LANES = 2 * HEAD
COLS = 512
CHUNK = 1024
TILE = 512
LOW = -1e30
SAFE = 80.0


def exchange(x):
    return lax.all_to_all(x, "tm", split_axis=0, concat_axis=0, tiled=True)


def low_lanes(shape):
    return lax.broadcasted_iota(jnp.int32, shape, len(shape) - 1) < HEAD


def swap(x):
    return pltpu.roll(x, HEAD, x.ndim - 1)


def normed_rows(x_ref, gain_ref):
    x = x_ref[...].astype(jnp.float32)
    x = jnp.concatenate([x[:, step] for step in range(x.shape[1])], axis=0)
    meansq = jnp.mean(x * x, axis=-1, keepdims=True)
    return (x * lax.rsqrt(meansq + 1e-06) * gain_ref[...]).astype(jnp.bfloat16)


def put_key_value(normed, wk_ref, wv_ref, out_ref):
    rows = normed.shape[0]
    k = jnp.dot(normed, wk_ref[...], preferred_element_type=jnp.float32)
    v = jnp.dot(normed, wv_ref[...], preferred_element_type=jnp.float32)
    for p in range(COLS // LANES):
        cols = slice(p * LANES, (p + 1) * LANES)
        kt, vt = k[:, cols], v[:, cols]
        low = low_lanes(kt.shape)
        out_ref[2 * p, :rows] = jnp.where(low, kt, swap(vt)).astype(jnp.bfloat16)
        out_ref[2 * p + 1, :rows] = jnp.where(low, swap(kt), vt).astype(jnp.bfloat16)


def own_kernel(x_ref, gain_ref, wk_ref, wv_ref, wq_ref, out_ref, normed_ref):
    @pl.when(pl.program_id(0) == 0)
    def _():
        normed_ref[...] = normed_rows(x_ref, gain_ref)

    normed = normed_ref[...]
    rows = normed.shape[0]
    half = rows // 2
    put_key_value(normed, wk_ref, wv_ref, out_ref)
    q = jnp.dot(normed, wq_ref[...], preferred_element_type=jnp.float32)
    q = q * (math.log2(math.e) / HEAD**0.5)
    for p in range(COLS // LANES):
        cols = slice(p * LANES, (p + 1) * LANES)
        top, bottom = q[:half, cols], q[half:, cols]
        low = low_lanes(top.shape)
        out_ref[2 * p, rows:] = jnp.where(low, top, swap(bottom)).astype(jnp.bfloat16)
        out_ref[2 * p + 1, rows:] = jnp.where(low, swap(top), bottom).astype(jnp.bfloat16)


def norm_kernel(x_ref, gain_ref, out_ref):
    out_ref[...] = normed_rows(x_ref, gain_ref)


def other_kernel(normed_ref, wk_ref, wv_ref, out_ref):
    put_key_value(normed_ref[...], wk_ref, wv_ref, out_ref)


def normalise(x, gain):
    var_rows, step_rows, width = x.shape
    return pl.pallas_call(
        norm_kernel,
        out_shape=jax.ShapeDtypeStruct((var_rows * step_rows, width), jnp.bfloat16),
        cost_estimate=pl.CostEstimate(flops=1 << 23, bytes_accessed=1 << 20, transcendentals=0),
        name="norm_other",
    )(x, gain)


def project_tokens(kernel, name, rows, out_rows, width, weights, first, specs, scratch, limit):
    return pl.pallas_call(
        kernel,
        grid=(width // COLS,),
        in_specs=specs + [pl.BlockSpec((width, COLS), lambda j: (0, j))] * len(weights),
        out_specs=pl.BlockSpec((COLS // HEAD, out_rows, LANES), lambda j: (j, 0, 0)),
        out_shape=jax.ShapeDtypeStruct((HEADS, out_rows, LANES), jnp.bfloat16),
        scratch_shapes=scratch,
        compiler_params=pltpu.CompilerParams(vmem_limit_bytes=limit << 20),
        cost_estimate=pl.CostEstimate(
            flops=2 * rows * width * width * len(weights),
            bytes_accessed=2 * width * width * len(weights) + 4 * rows * width,
            transcendentals=0,
        ),
        name=name,
    )(*first, *weights)


def project_own(x, gain, weights):
    var_rows, step_rows, width = x.shape
    rows = var_rows * step_rows
    specs = [
        pl.BlockSpec(x.shape, lambda j: (0, 0, 0)),
        pl.BlockSpec((1, width), lambda j: (0, 0)),
    ]
    scratch = [pltpu.VMEM((rows, width), jnp.bfloat16)]
    return project_tokens(
        own_kernel, "project_own", rows, rows * 3 // 2, width, weights, (x, gain), specs, scratch, 56
    )


def project_other(normed, weights):
    rows, width = normed.shape
    specs = [pl.BlockSpec((rows, width), lambda j: (0, 0))]
    return project_tokens(
        other_kernel, "project_other", rows, rows, width, weights, (normed,), specs, [], 20
    )


def attend_kernel(final, *refs):
    q_ref, *refs = refs
    kv_ref = q_ref
    if final:
        q_far = q_ref
        kv_ref, state_in, longest_in, out_ref, q_ref, sem, acc, *refs = refs
        fetch = pltpu.make_async_copy(q_far.at[:, kv_ref.shape[1] :], q_ref, sem.at[0])
        fetch.start()
    else:
        acc, longest_out, *refs = refs
    top, query, key, value, p0, p1, query_len, key_len = refs
    rows = kv_ref.shape[1] if final else q_ref.shape[1] * 2 // 3
    half = rows // 2
    per = TILE // rows
    tiles = HEADS // per
    lane_of = lambda axis: lax.broadcasted_iota(jnp.int32, (LANES, LANES), axis) // HEAD
    same_half = (lane_of(0) == lane_of(1)).astype(jnp.bfloat16)
    key_half = (lane_of(0) == 0).astype(jnp.bfloat16)

    def lengths(x, ones):
        return jnp.dot((x * x).astype(jnp.bfloat16), ones, preferred_element_type=jnp.float32)

    def at(tile, count=1):
        return pl.ds(pl.multiple_of(tile * TILE, TILE), count * TILE)

    def prepare_queries(t, carry):
        x = q_ref[t, (0 if final else rows) :].astype(jnp.float32)
        if not final:
            query_len[...] = jnp.maximum(query_len[...], lengths(x, same_half))
        low = low_lanes(x.shape)
        lane = lax.broadcasted_iota(jnp.int32, x.shape, 1) - HEAD
        for part, y in enumerate((x, swap(x))):
            step = 2 * (t % per) + part
            later = jnp.where((lane > step) & (lane < 2 * per), LOW, jnp.float32(0.0))
            first = jnp.where(t // per % 2 == 0, later, 0.0)
            to = pl.ds(pl.multiple_of(t * rows + part * half, half), half)
            for n, mask in enumerate((0.0, first, later)):
                query[n, to] = jnp.where(low, y, mask).astype(jnp.bfloat16)
        return carry

    def prepare(t, carry):
        block = pl.ds(pl.multiple_of(t * rows, rows), rows)
        kv = kv_ref[t, :rows].astype(jnp.float32)
        key_len[...] = jnp.maximum(key_len[...], lengths(kv, key_half))
        low = low_lanes(kv.shape)
        lane = lax.broadcasted_iota(jnp.int32, kv.shape, 1) - HEAD
        step = 2 * (t % per) + lax.broadcasted_iota(jnp.int32, kv.shape, 0) // half
        is_step = jnp.where(lane == step, jnp.float32(1.0), jnp.float32(0.0))
        key[block] = jnp.where(low, kv, is_step).astype(jnp.bfloat16)
        value[block] = jnp.where(low, 1.0, kv).astype(jnp.bfloat16)
        acc[block] = state_in[block] if final else jnp.zeros((rows, LANES), jnp.float32)
        return carry

    query_len[...] = jnp.zeros_like(query_len)
    key_len[...] = jnp.zeros_like(key_len)
    lax.fori_loop(0, HEADS, prepare, 0, unroll=2)
    if final:
        fetch.wait()
    lax.fori_loop(0, HEADS, prepare_queries, 0, unroll=2)
    longest = longest_in[0] if final else jnp.max(query_len[...])
    fits = longest * jnp.max(key_len[...]) <= SAFE * SAFE
    if final:
        own_fits = longest >= 0.0
        fits = fits & own_fits
    else:
        longest_out[0] = jnp.where(fits, longest, -1.0)

    def scores(q, j):
        return lax.dot_general(
            q, key[at(j)], (((1,), (1,)), ((), ())), preferred_element_type=jnp.float32
        )

    def weighted(p, j):
        return jnp.dot(p, value[at(j)], preferred_element_type=jnp.float32)

    @pl.when(fits)
    def _():
        def weights(p, j, first):
            diagonal = (j == first).astype(jnp.int32)
            p[...] = jnp.exp2(scores(query[diagonal, at(first, 2)], j)).astype(jnp.bfloat16)

        def gather(p, j, first):
            acc[at(first, 2)] += weighted(p[...], j)

        def late_weights(p, j):
            p[:TILE] = jnp.exp2(scores(query[2, at(j)], j)).astype(jnp.bfloat16)

        def late_gather(p, j):
            acc[at(j)] += weighted(p[:TILE], j)

        def chunk(a, carry):
            first = 2 * a

            def turn(n, carry):
                j = 2 * n
                weights(p1, j + 1, first)
                gather(p0, j, first)
                weights(p0, j + 2, first)
                gather(p1, j + 1, first)
                return carry

            lax.fori_loop(0, a, turn, 0)
            late_weights(p1, first + 1)
            gather(p0, first, first)
            weights(p0, jnp.int32(0), jnp.minimum(first + 2, tiles - 2))
            late_gather(p1, first + 1)
            return carry

        weights(p0, jnp.int32(0), jnp.int32(0))
        lax.fori_loop(0, tiles // 2, chunk, 0)

    @pl.when(jnp.logical_not(fits))
    def _():
        lane = lax.broadcasted_iota(jnp.int32, (TILE, LANES), 1)

        def spread(x, n):
            return jnp.max(jnp.where(lane == n, x, -jnp.inf), axis=-1, keepdims=True)

        def row_block(i, carry):
            to = at(i)
            if final:
                x = acc[to]
                top[...] = jnp.where(own_fits, 0.0, spread(x, HEAD // 2)) + jnp.zeros_like(x)
                acc[to] = jnp.where(lane < HEAD, spread(x, 0), x)
            else:
                top[...] = jnp.full_like(top, LOW)

            def key_block(j, carry):
                s = scores(query[2 * (i == j).astype(jnp.int32), to], j)
                old = top[...]
                new = jnp.maximum(old, jnp.max(s, axis=-1, keepdims=True))
                p = jnp.exp2(s - jnp.concatenate([new] * (TILE // LANES), axis=1))
                acc[to] = acc[to] * jnp.exp2(old - new) + weighted(p.astype(jnp.bfloat16), j)
                top[...] = new
                return carry

            lax.fori_loop(0, i + 1, key_block, 0)
            if not final:
                x = acc[to]
                acc[to] = jnp.where((lane >= HEAD // 2) & (lane < HEAD), top[...], x)
            return carry

        lax.fori_loop(0, tiles, row_block, 0)

    if final:

        def finish(t, carry):
            base = pl.multiple_of(t * rows, rows)
            x = acc[pl.ds(base, half)]
            y = acc[pl.ds(base + half, half)]
            low = low_lanes(x.shape)
            num = jnp.where(low, swap(x), y)
            den = jnp.where(low, x, swap(y))
            out_ref[t] = (num / den).astype(jnp.bfloat16)
            return carry

        lax.fori_loop(0, HEADS, finish, 0, unroll=2)


def attend(*operands):
    rows = operands[0].shape[1] * 2 // 3
    final = len(operands) > 1
    total = HEADS * rows
    whole = pl.BlockSpec(memory_space=pltpu.VMEM)
    scalar = pl.BlockSpec(memory_space=pltpu.SMEM)
    far = pl.BlockSpec(memory_space=pl.ANY)
    bf16_rows = pltpu.VMEM((total, LANES), jnp.bfloat16)
    f32_rows = pltpu.VMEM((total, LANES), jnp.float32)
    scratch = [
        pltpu.VMEM((HEADS, rows // 2, LANES), jnp.bfloat16),
        pltpu.SemaphoreType.DMA((1,)),
        f32_rows,
    ] * final + [
        pltpu.VMEM((TILE, LANES), jnp.float32),
        pltpu.VMEM((3, total, LANES), jnp.bfloat16),
        bf16_rows,
        bf16_rows,
        pltpu.VMEM((CHUNK, TILE), jnp.bfloat16),
        pltpu.VMEM((CHUNK, TILE), jnp.bfloat16),
        pltpu.VMEM((rows // 2, LANES), jnp.float32),
        pltpu.VMEM((rows, LANES), jnp.float32),
    ]
    if final:
        out = jax.ShapeDtypeStruct((HEADS, rows // 2, LANES), jnp.bfloat16)
    else:
        out = [
            jax.ShapeDtypeStruct((total, LANES), jnp.float32),
            jax.ShapeDtypeStruct((1,), jnp.float32),
        ]
    pairs = total * total // 2
    return pl.pallas_call(
        functools.partial(attend_kernel, final),
        in_specs=[far, whole, whole, scalar] if final else [whole],
        out_specs=whole if final else [whole, scalar],
        out_shape=out,
        scratch_shapes=scratch,
        compiler_params=pltpu.CompilerParams(vmem_limit_bytes=20 << 20),
        cost_estimate=pl.CostEstimate(
            flops=16 * pairs * LANES, bytes_accessed=8 << 20, transcendentals=pairs
        ),
        name="attend_other" if final else "attend_own",
    )(*operands)


def out_kernel(a_ref, w_ref, o_ref, flat):
    half = a_ref.shape[1]

    for p in range(HEADS // 2):
        a = a_ref[2 * p].astype(jnp.float32)
        b = a_ref[2 * p + 1].astype(jnp.float32)
        low = low_lanes(a.shape)
        cols = slice(p * LANES, (p + 1) * LANES)
        flat[:half, cols] = jnp.where(low, a, swap(b)).astype(jnp.bfloat16)
        flat[half:, cols] = jnp.where(low, swap(a), b).astype(jnp.bfloat16)
    for c in range(0, w_ref.shape[1], COLS):
        mixed = jnp.dot(flat[...], w_ref[:, c : c + COLS], preferred_element_type=jnp.float32)
        mixed = [mixed[step * half : (step + 1) * half] for step in range(2)]
        o_ref[:, :, c : c + COLS] = jnp.stack(mixed, axis=1).astype(jnp.bfloat16)


def project_out(att, w_out):
    half = att.shape[1]
    width = w_out.shape[0]
    rows = 2 * half
    return pl.pallas_call(
        out_kernel,
        in_specs=[pl.BlockSpec(memory_space=pltpu.VMEM)] * 2,
        out_specs=pl.BlockSpec(memory_space=pltpu.VMEM),
        out_shape=jax.ShapeDtypeStruct((half, 2, width), jnp.bfloat16),
        scratch_shapes=[pltpu.VMEM((rows, width), jnp.bfloat16)],
        compiler_params=pltpu.CompilerParams(vmem_limit_bytes=24 << 20),
        cost_estimate=pl.CostEstimate(
            flops=2 * rows * width * width, bytes_accessed=2 * width * width, transcendentals=0
        ),
        name="project_out",
    )(att, w_out)


def block_for(adjacency, mine):
    blocks = jnp.arange(adjacency.shape[0], dtype=jnp.int32)
    row = lax.dynamic_index_in_dim(adjacency, mine, 0, keepdims=False)
    others = row * (blocks != mine).astype(jnp.int32)
    return jnp.sum(others * blocks) + (1 - jnp.sum(others)) * mine


def choose(index, options):
    return functools.reduce(
        lambda rest, at: jnp.where(index == at, options[at], rest),
        range(len(options) - 1),
        options[-1],
    )


def same_core(x):
    count = lax.axis_size("var")
    held = []
    for offset in range(1, count // 2):
        pairs = [(v, (v + 2 * offset) % count) for v in range(count)]
        held.append(lax.ppermute(x, "var", pairs))
    return held


def pick_other(held, adjacency):
    count = lax.axis_size("var")
    chips = count // 2
    mine = lax.axis_index("var")
    want = block_for(adjacency, mine)
    partner_want = block_for(adjacency, mine ^ 1)
    away = lambda block: (mine // 2 - block // 2 + chips) % chips
    to_send = choose(away(partner_want), held)
    got = lax.ppermute(to_send, "var", [(v, v ^ 1) for v in range(count)])
    slot = jnp.where(want % 2 == mine % 2, away(want), chips)
    return choose(slot, held + [got])


def local(tokens, gain, w_query, w_key, w_value, w_out, adjacency):
    gain = gain.reshape(1, -1)
    held = same_core(tokens)
    packed = project_own(tokens, gain, (w_key, w_value, w_query))
    *held, _ = lax.optimization_barrier((*held, packed))
    x_other = pick_other([tokens, *held], adjacency)
    kv_other = project_other(normalise(x_other, gain), (w_key, w_value))
    packed, _ = lax.optimization_barrier((exchange(packed), kv_other))
    kv_other = exchange(kv_other)
    att = exchange(attend(packed, kv_other, *attend(packed)))
    return project_out(att, w_out)


def solution(mesh):
    in_specs = (P("var", "tm", None), P(), P(), P(), P(), P(), P())
    out_specs = P("var", "tm", None)
    return jax.shard_map(local, mesh=mesh, in_specs=in_specs, out_specs=out_specs, check_vma=False)
```

```python
import functools
import math

import jax
import jax.numpy as jnp
from jax import lax
from jax.experimental import pallas as pl
from jax.experimental.pallas import tpu as pltpu
from jax.sharding import PartitionSpec as P

HEADS = 16
HEAD = 64
LANES = 2 * HEAD
COLS = 512
CHUNK = 1024
TILE = 512
LOW = -1e30
SAFE = 80.0


def exchange(x):
    return lax.all_to_all(x, "tm", split_axis=0, concat_axis=0, tiled=True)


def low_lanes(shape):
    return lax.broadcasted_iota(jnp.int32, shape, len(shape) - 1) < HEAD


def swap(x):
    return pltpu.roll(x, HEAD, x.ndim - 1)


def normed_rows(x_ref, gain_ref):
    x = x_ref[...].astype(jnp.float32)
    x = jnp.concatenate([x[:, step] for step in range(x.shape[1])], axis=0)
    meansq = jnp.mean(x * x, axis=-1, keepdims=True)
    return (x * lax.rsqrt(meansq + 1e-06) * gain_ref[...]).astype(jnp.bfloat16)


def project_kernel(with_query, *refs):
    x_ref, gain_ref, wk_ref, wv_ref = refs[:4]
    out_ref, normed_ref = refs[-2:]
    step = pl.program_id(0)

    @pl.when(step == 0)
    def _():
        normed_ref[...] = normed_rows(x_ref, gain_ref)

    normed = normed_ref[...]
    rows = normed.shape[0]
    half = rows // 2
    k = jnp.dot(normed, wk_ref[...], preferred_element_type=jnp.float32)
    v = jnp.dot(normed, wv_ref[...], preferred_element_type=jnp.float32)
    if with_query:
        q = jnp.dot(normed, refs[4][...], preferred_element_type=jnp.float32)
        q = q * (math.log2(math.e) / HEAD**0.5)
    for p in range(COLS // LANES):
        cols = slice(p * LANES, (p + 1) * LANES)
        kt, vt = k[:, cols], v[:, cols]
        low = low_lanes(kt.shape)
        out_ref[2 * p, :rows] = jnp.where(low, kt, swap(vt)).astype(jnp.bfloat16)
        out_ref[2 * p + 1, :rows] = jnp.where(low, swap(kt), vt).astype(jnp.bfloat16)
        if with_query:
            top, bottom = q[:half, cols], q[half:, cols]
            low = low_lanes(top.shape)
            out_ref[2 * p, rows:] = jnp.where(low, top, swap(bottom)).astype(jnp.bfloat16)
            out_ref[2 * p + 1, rows:] = jnp.where(low, swap(top), bottom).astype(jnp.bfloat16)


def project(x, gain, weights):
    var_rows, step_rows, width = x.shape
    rows = var_rows * step_rows
    with_query = len(weights) == 3
    out_rows = rows + rows // 2 if with_query else rows
    flops = 2 * rows * width * width * len(weights)
    return pl.pallas_call(
        functools.partial(project_kernel, with_query),
        grid=(width // COLS,),
        in_specs=[
            pl.BlockSpec(x.shape, lambda j: (0, 0, 0)),
            pl.BlockSpec((1, width), lambda j: (0, 0)),
        ]
        + [pl.BlockSpec((width, COLS), lambda j: (0, j))] * len(weights),
        out_specs=pl.BlockSpec((COLS // HEAD, out_rows, LANES), lambda j: (j, 0, 0)),
        out_shape=jax.ShapeDtypeStruct((HEADS, out_rows, LANES), jnp.bfloat16),
        scratch_shapes=[pltpu.VMEM((rows, width), jnp.bfloat16)],
        compiler_params=pltpu.CompilerParams(vmem_limit_bytes=(56 if with_query else 20) << 20),
        cost_estimate=pl.CostEstimate(
            flops=flops, bytes_accessed=2 * width * width * len(weights) + 4 * rows * width,
            transcendentals=0,
        ),
        name="project_own" if with_query else "project_other",
    )(x, gain, *weights)


def attend_kernel(final, *refs):
    q_ref, *refs = refs
    kv_ref = q_ref
    if final:
        q_far = q_ref
        kv_ref, state_in, longest_in, out_ref, q_ref, sem, acc, *refs = refs
        fetch = pltpu.make_async_copy(q_far.at[:, kv_ref.shape[1] :], q_ref, sem.at[0])
        fetch.start()
    else:
        acc, longest_out, *refs = refs
    top, query, key, value, p0, p1, query_len, key_len = refs
    rows = kv_ref.shape[1] if final else q_ref.shape[1] * 2 // 3
    half = rows // 2
    per = TILE // rows
    tiles = HEADS // per
    lane_of = lambda axis: lax.broadcasted_iota(jnp.int32, (LANES, LANES), axis) // HEAD
    same_half = (lane_of(0) == lane_of(1)).astype(jnp.bfloat16)
    key_half = (lane_of(0) == 0).astype(jnp.bfloat16)

    def lengths(x, ones):
        return jnp.dot((x * x).astype(jnp.bfloat16), ones, preferred_element_type=jnp.float32)

    def at(tile, count=1):
        return pl.ds(pl.multiple_of(tile * TILE, TILE), count * TILE)

    def prepare_queries(t, carry):
        x = q_ref[t, (0 if final else rows) :].astype(jnp.float32)
        if not final:
            query_len[...] = jnp.maximum(query_len[...], lengths(x, same_half))
        low = low_lanes(x.shape)
        lane = lax.broadcasted_iota(jnp.int32, x.shape, 1) - HEAD
        for part, y in enumerate((x, swap(x))):
            step = 2 * (t % per) + part
            later = jnp.where((lane > step) & (lane < 2 * per), LOW, jnp.float32(0.0))
            first = jnp.where(t // per % 2 == 0, later, 0.0)
            to = pl.ds(pl.multiple_of(t * rows + part * half, half), half)
            for n, mask in enumerate((0.0, first, later)):
                query[n, to] = jnp.where(low, y, mask).astype(jnp.bfloat16)
        return carry

    def prepare(t, carry):
        block = pl.ds(pl.multiple_of(t * rows, rows), rows)
        kv = kv_ref[t, :rows].astype(jnp.float32)
        key_len[...] = jnp.maximum(key_len[...], lengths(kv, key_half))
        low = low_lanes(kv.shape)
        lane = lax.broadcasted_iota(jnp.int32, kv.shape, 1) - HEAD
        step = 2 * (t % per) + lax.broadcasted_iota(jnp.int32, kv.shape, 0) // half
        is_step = jnp.where(lane == step, jnp.float32(1.0), jnp.float32(0.0))
        key[block] = jnp.where(low, kv, is_step).astype(jnp.bfloat16)
        value[block] = jnp.where(low, 1.0, kv).astype(jnp.bfloat16)
        acc[block] = state_in[block] if final else jnp.zeros((rows, LANES), jnp.float32)
        return carry

    query_len[...] = jnp.zeros_like(query_len)
    key_len[...] = jnp.zeros_like(key_len)
    if final:
        lax.fori_loop(0, HEADS, prepare, 0, unroll=4)
        fetch.wait()
        lax.fori_loop(0, HEADS, prepare_queries, 0, unroll=4)
    else:
        both = lambda t, carry: prepare(t, prepare_queries(t, carry))
        lax.fori_loop(0, HEADS, both, 0, unroll=4)
    longest = longest_in[0] if final else jnp.max(query_len[...])
    fits = longest * jnp.max(key_len[...]) <= SAFE * SAFE
    if final:
        own_fits = longest >= 0.0
        fits = fits & own_fits
    else:
        longest_out[0] = jnp.where(fits, longest, -1.0)

    def scores(q, j):
        return lax.dot_general(
            q, key[at(j)], (((1,), (1,)), ((), ())), preferred_element_type=jnp.float32
        )

    def weighted(p, j):
        return jnp.dot(p, value[at(j)], preferred_element_type=jnp.float32)

    @pl.when(fits)
    def _():
        def weights(p, j, first):
            diagonal = (j == first).astype(jnp.int32)
            p[...] = jnp.exp2(scores(query[diagonal, at(first, 2)], j)).astype(jnp.bfloat16)

        def gather(p, j, first):
            acc[at(first, 2)] += weighted(p[...], j)

        def late_weights(p, j):
            p[:TILE] = jnp.exp2(scores(query[2, at(j)], j)).astype(jnp.bfloat16)

        def late_gather(p, j):
            acc[at(j)] += weighted(p[:TILE], j)

        def chunk(a, carry):
            first = 2 * a

            def turn(n, carry):
                j = 2 * n
                weights(p1, j + 1, first)
                gather(p0, j, first)
                weights(p0, j + 2, first)
                gather(p1, j + 1, first)
                return carry

            lax.fori_loop(0, a, turn, 0)
            late_weights(p1, first + 1)
            gather(p0, first, first)
            weights(p0, jnp.int32(0), jnp.minimum(first + 2, tiles - 2))
            late_gather(p1, first + 1)
            return carry

        weights(p0, jnp.int32(0), jnp.int32(0))
        lax.fori_loop(0, tiles // 2, chunk, 0)

    @pl.when(jnp.logical_not(fits))
    def _():
        lane = lax.broadcasted_iota(jnp.int32, (TILE, LANES), 1)

        def spread(x, n):
            return jnp.max(jnp.where(lane == n, x, -jnp.inf), axis=-1, keepdims=True)

        def row_block(i, carry):
            to = at(i)
            if final:
                x = acc[to]
                top[...] = jnp.where(own_fits, 0.0, spread(x, HEAD // 2)) + jnp.zeros_like(x)
                acc[to] = jnp.where(lane < HEAD, spread(x, 0), x)
            else:
                top[...] = jnp.full_like(top, LOW)

            def key_block(j, carry):
                s = scores(query[2 * (i == j).astype(jnp.int32), to], j)
                old = top[...]
                new = jnp.maximum(old, jnp.max(s, axis=-1, keepdims=True))
                p = jnp.exp2(s - jnp.concatenate([new] * (TILE // LANES), axis=1))
                acc[to] = acc[to] * jnp.exp2(old - new) + weighted(p.astype(jnp.bfloat16), j)
                top[...] = new
                return carry

            lax.fori_loop(0, i + 1, key_block, 0)
            if not final:
                x = acc[to]
                acc[to] = jnp.where((lane >= HEAD // 2) & (lane < HEAD), top[...], x)
            return carry

        lax.fori_loop(0, tiles, row_block, 0)

    if final:

        def finish(t, carry):
            base = pl.multiple_of(t * rows, rows)
            x = acc[pl.ds(base, half)]
            y = acc[pl.ds(base + half, half)]
            low = low_lanes(x.shape)
            num = jnp.where(low, swap(x), y)
            den = jnp.where(low, x, swap(y))
            out_ref[t] = (num / den).astype(jnp.bfloat16)
            return carry

        lax.fori_loop(0, HEADS, finish, 0, unroll=4)


def attend(*operands):
    rows = operands[0].shape[1] * 2 // 3
    final = len(operands) > 1
    total = HEADS * rows
    whole = pl.BlockSpec(memory_space=pltpu.VMEM)
    scalar = pl.BlockSpec(memory_space=pltpu.SMEM)
    far = pl.BlockSpec(memory_space=pl.ANY)
    bf16_rows = pltpu.VMEM((total, LANES), jnp.bfloat16)
    f32_rows = pltpu.VMEM((total, LANES), jnp.float32)
    scratch = [
        pltpu.VMEM((HEADS, rows // 2, LANES), jnp.bfloat16),
        pltpu.SemaphoreType.DMA((1,)),
        f32_rows,
    ] * final + [
        pltpu.VMEM((TILE, LANES), jnp.float32),
        pltpu.VMEM((3, total, LANES), jnp.bfloat16),
        bf16_rows,
        bf16_rows,
        pltpu.VMEM((CHUNK, TILE), jnp.bfloat16),
        pltpu.VMEM((CHUNK, TILE), jnp.bfloat16),
        pltpu.VMEM((rows // 2, LANES), jnp.float32),
        pltpu.VMEM((rows, LANES), jnp.float32),
    ]
    if final:
        out = jax.ShapeDtypeStruct((HEADS, rows // 2, LANES), jnp.bfloat16)
    else:
        out = [
            jax.ShapeDtypeStruct((total, LANES), jnp.float32),
            jax.ShapeDtypeStruct((1,), jnp.float32),
        ]
    pairs = total * total // 2
    return pl.pallas_call(
        functools.partial(attend_kernel, final),
        in_specs=[far, whole, whole, scalar] if final else [whole],
        out_specs=whole if final else [whole, scalar],
        out_shape=out,
        scratch_shapes=scratch,
        compiler_params=pltpu.CompilerParams(vmem_limit_bytes=20 << 20),
        cost_estimate=pl.CostEstimate(
            flops=16 * pairs * LANES, bytes_accessed=8 << 20, transcendentals=pairs
        ),
        name="attend_other" if final else "attend_own",
    )(*operands)


def out_kernel(a_ref, w_ref, o_ref, flat):
    half = a_ref.shape[1]

    for p in range(HEADS // 2):
        a = a_ref[2 * p].astype(jnp.float32)
        b = a_ref[2 * p + 1].astype(jnp.float32)
        low = low_lanes(a.shape)
        cols = slice(p * LANES, (p + 1) * LANES)
        flat[:half, cols] = jnp.where(low, a, swap(b)).astype(jnp.bfloat16)
        flat[half:, cols] = jnp.where(low, swap(a), b).astype(jnp.bfloat16)
    for c in range(0, w_ref.shape[1], COLS):
        mixed = jnp.dot(flat[...], w_ref[:, c : c + COLS], preferred_element_type=jnp.float32)
        mixed = [mixed[step * half : (step + 1) * half] for step in range(2)]
        o_ref[:, :, c : c + COLS] = jnp.stack(mixed, axis=1).astype(jnp.bfloat16)


def project_out(att, w_out):
    half = att.shape[1]
    width = w_out.shape[0]
    rows = 2 * half
    return pl.pallas_call(
        out_kernel,
        in_specs=[pl.BlockSpec(memory_space=pltpu.VMEM)] * 2,
        out_specs=pl.BlockSpec(memory_space=pltpu.VMEM),
        out_shape=jax.ShapeDtypeStruct((half, 2, width), jnp.bfloat16),
        scratch_shapes=[pltpu.VMEM((rows, width), jnp.bfloat16)],
        compiler_params=pltpu.CompilerParams(vmem_limit_bytes=24 << 20),
        cost_estimate=pl.CostEstimate(
            flops=2 * rows * width * width, bytes_accessed=2 * width * width, transcendentals=0
        ),
        name="project_out",
    )(att, w_out)


def block_for(adjacency, mine):
    blocks = jnp.arange(adjacency.shape[0], dtype=jnp.int32)
    row = lax.dynamic_index_in_dim(adjacency, mine, 0, keepdims=False)
    others = row * (blocks != mine).astype(jnp.int32)
    return jnp.sum(others * blocks) + (1 - jnp.sum(others)) * mine


def choose(index, options):
    return functools.reduce(
        lambda rest, at: jnp.where(index == at, options[at], rest),
        range(len(options) - 1),
        options[-1],
    )


def same_core(x):
    count = lax.axis_size("var")
    held = []
    for offset in range(1, count // 2):
        pairs = [(v, (v + 2 * offset) % count) for v in range(count)]
        held.append(lax.ppermute(x, "var", pairs))
    return held


def pick_other(held, adjacency):
    count = lax.axis_size("var")
    chips = count // 2
    mine = lax.axis_index("var")
    want = block_for(adjacency, mine)
    partner_want = block_for(adjacency, mine ^ 1)
    away = lambda block: (mine // 2 - block // 2 + chips) % chips
    to_send = choose(away(partner_want), held)
    got = lax.ppermute(to_send, "var", [(v, v ^ 1) for v in range(count)])
    slot = jnp.where(want % 2 == mine % 2, away(want), chips)
    return choose(slot, held + [got])


def local(tokens, gain, w_query, w_key, w_value, w_out, adjacency):
    gain = gain.reshape(1, -1)
    held = same_core(tokens)
    packed = project(tokens, gain, (w_key, w_value, w_query))
    *held, _ = lax.optimization_barrier((*held, packed))
    x_other = pick_other([tokens, *held], adjacency)
    kv_other = project(x_other, gain, (w_key, w_value))
    packed, _ = lax.optimization_barrier((exchange(packed), kv_other))
    kv_other = exchange(kv_other)
    att = exchange(attend(packed, kv_other, *attend(packed)))
    return project_out(att, w_out)


def solution(mesh):
    in_specs = (P("var", "tm", None), P(), P(), P(), P(), P(), P())
    out_specs = P("var", "tm", None)
    return jax.shard_map(local, mesh=mesh, in_specs=in_specs, out_specs=out_specs, check_vma=False)
```

```python
import functools
import math

import jax
import jax.numpy as jnp
from jax import lax
from jax.experimental import pallas as pl
from jax.experimental.pallas import tpu as pltpu
from jax.sharding import PartitionSpec as P

HEADS = 16
HEAD = 64
LANES = 2 * HEAD
COLS = 512
CHUNK = 1024
TILE = 512
LOW = -1e30
SAFE = 80.0


def exchange(x):
    return lax.all_to_all(x, "tm", split_axis=0, concat_axis=0, tiled=True)


def low_lanes(shape):
    return lax.broadcasted_iota(jnp.int32, shape, len(shape) - 1) < HEAD


def swap(x):
    return pltpu.roll(x, HEAD, x.ndim - 1)


def normed_rows(x_ref, gain_ref):
    x = x_ref[...].astype(jnp.float32)
    x = jnp.concatenate([x[:, step] for step in range(x.shape[1])], axis=0)
    meansq = jnp.mean(x * x, axis=-1, keepdims=True)
    return (x * lax.rsqrt(meansq + 1e-06) * gain_ref[...]).astype(jnp.bfloat16)


def project_kernel(with_query, *refs):
    x_ref, gain_ref, wk_ref, wv_ref = refs[:4]
    out_ref, normed_ref = refs[-2:]
    step = pl.program_id(0)

    @pl.when(step == 0)
    def _():
        normed_ref[...] = normed_rows(x_ref, gain_ref)

    normed = normed_ref[...]
    rows = normed.shape[0]
    half = rows // 2
    k = jnp.dot(normed, wk_ref[...], preferred_element_type=jnp.float32)
    v = jnp.dot(normed, wv_ref[...], preferred_element_type=jnp.float32)
    if with_query:
        q = jnp.dot(normed, refs[4][...], preferred_element_type=jnp.float32)
        q = q * (math.log2(math.e) / HEAD**0.5)
    for p in range(COLS // LANES):
        cols = slice(p * LANES, (p + 1) * LANES)
        kt, vt = k[:, cols], v[:, cols]
        low = low_lanes(kt.shape)
        out_ref[2 * p, :rows] = jnp.where(low, kt, swap(vt)).astype(jnp.bfloat16)
        out_ref[2 * p + 1, :rows] = jnp.where(low, swap(kt), vt).astype(jnp.bfloat16)
        if with_query:
            top, bottom = q[:half, cols], q[half:, cols]
            low = low_lanes(top.shape)
            out_ref[2 * p, rows:] = jnp.where(low, top, swap(bottom)).astype(jnp.bfloat16)
            out_ref[2 * p + 1, rows:] = jnp.where(low, swap(top), bottom).astype(jnp.bfloat16)


def project(x, gain, weights):
    var_rows, step_rows, width = x.shape
    rows = var_rows * step_rows
    with_query = len(weights) == 3
    out_rows = rows + rows // 2 if with_query else rows
    flops = 2 * rows * width * width * len(weights)
    return pl.pallas_call(
        functools.partial(project_kernel, with_query),
        grid=(width // COLS,),
        in_specs=[
            pl.BlockSpec(x.shape, lambda j: (0, 0, 0)),
            pl.BlockSpec((1, width), lambda j: (0, 0)),
        ]
        + [pl.BlockSpec((width, COLS), lambda j: (0, j))] * len(weights),
        out_specs=pl.BlockSpec((COLS // HEAD, out_rows, LANES), lambda j: (j, 0, 0)),
        out_shape=jax.ShapeDtypeStruct((HEADS, out_rows, LANES), jnp.bfloat16),
        scratch_shapes=[pltpu.VMEM((rows, width), jnp.bfloat16)],
        compiler_params=pltpu.CompilerParams(vmem_limit_bytes=(56 if with_query else 20) << 20),
        cost_estimate=pl.CostEstimate(
            flops=flops, bytes_accessed=2 * width * width * len(weights) + 4 * rows * width,
            transcendentals=0,
        ),
        name="project_own" if with_query else "project_other",
    )(x, gain, *weights)


def attend_kernel(final, *refs):
    q_ref, *refs = refs
    kv_ref = q_ref
    if final:
        q_far = q_ref
        kv_ref, state_in, longest_in, out_ref, q_ref, sem, acc, *refs = refs
        fetch = pltpu.make_async_copy(q_far.at[:, kv_ref.shape[1] :], q_ref, sem.at[0])
        fetch.start()
    else:
        acc, longest_out, *refs = refs
    top, query, key, value, p0, p1, query_len, key_len = refs
    rows = kv_ref.shape[1] if final else q_ref.shape[1] * 2 // 3
    half = rows // 2
    per = TILE // rows
    tiles = HEADS // per
    lane_of = lambda axis: lax.broadcasted_iota(jnp.int32, (LANES, LANES), axis) // HEAD
    same_half = (lane_of(0) == lane_of(1)).astype(jnp.bfloat16)
    key_half = (lane_of(0) == 0).astype(jnp.bfloat16)

    def lengths(x, ones):
        return jnp.dot((x * x).astype(jnp.bfloat16), ones, preferred_element_type=jnp.float32)

    def at(tile, count=1):
        return pl.ds(pl.multiple_of(tile * TILE, TILE), count * TILE)

    def prepare_queries(t, carry):
        x = q_ref[t, (0 if final else rows) :].astype(jnp.float32)
        if not final:
            query_len[...] = jnp.maximum(query_len[...], lengths(x, same_half))
        low = low_lanes(x.shape)
        lane = lax.broadcasted_iota(jnp.int32, x.shape, 1) - HEAD
        for part, y in enumerate((x, swap(x))):
            step = 2 * (t % per) + part
            later = jnp.where((lane > step) & (lane < 2 * per), LOW, jnp.float32(0.0))
            first = jnp.where(t // per % 2 == 0, later, 0.0)
            to = pl.ds(pl.multiple_of(t * rows + part * half, half), half)
            for n, mask in enumerate((0.0, first, later)):
                query[n, to] = jnp.where(low, y, mask).astype(jnp.bfloat16)
        return carry

    def prepare(t, carry):
        block = pl.ds(pl.multiple_of(t * rows, rows), rows)
        kv = kv_ref[t, :rows].astype(jnp.float32)
        key_len[...] = jnp.maximum(key_len[...], lengths(kv, key_half))
        low = low_lanes(kv.shape)
        lane = lax.broadcasted_iota(jnp.int32, kv.shape, 1) - HEAD
        step = 2 * (t % per) + lax.broadcasted_iota(jnp.int32, kv.shape, 0) // half
        is_step = jnp.where(lane == step, jnp.float32(1.0), jnp.float32(0.0))
        key[block] = jnp.where(low, kv, is_step).astype(jnp.bfloat16)
        value[block] = jnp.where(low, 1.0, kv).astype(jnp.bfloat16)
        acc[block] = state_in[block] if final else jnp.zeros((rows, LANES), jnp.float32)
        return carry

    query_len[...] = jnp.zeros_like(query_len)
    key_len[...] = jnp.zeros_like(key_len)
    if final:
        lax.fori_loop(0, HEADS, prepare, 0, unroll=8)
        fetch.wait()
        lax.fori_loop(0, HEADS, prepare_queries, 0, unroll=8)
    else:
        both = lambda t, carry: prepare(t, prepare_queries(t, carry))
        lax.fori_loop(0, HEADS, both, 0, unroll=8)
    longest = longest_in[0] if final else jnp.max(query_len[...])
    fits = longest * jnp.max(key_len[...]) <= SAFE * SAFE
    if final:
        own_fits = longest >= 0.0
        fits = fits & own_fits
    else:
        longest_out[0] = jnp.where(fits, longest, -1.0)

    def scores(q, j):
        return lax.dot_general(
            q, key[at(j)], (((1,), (1,)), ((), ())), preferred_element_type=jnp.float32
        )

    def weighted(p, j):
        return jnp.dot(p, value[at(j)], preferred_element_type=jnp.float32)

    @pl.when(fits)
    def _():
        size = CHUNK // (4 if final else 2)

        def parts(first):
            for r in range(0, CHUNK, size):
                yield slice(r, r + size), pl.ds(pl.multiple_of(first * TILE + r, size), size)

        def weights(p, j, first):
            diagonal = (j == first).astype(jnp.int32)
            for here, to in parts(first):
                p[here] = jnp.exp2(scores(query[diagonal, to], j)).astype(jnp.bfloat16)

        def step(p_next, j_next, p, j, first):
            diagonal = (j_next == first).astype(jnp.int32)
            for here, to in parts(first):
                p_next[here] = jnp.exp2(scores(query[diagonal, to], j_next)).astype(jnp.bfloat16)
                acc[to] += weighted(p[here], j)

        def gather(p, j, first):
            acc[at(first, 2)] += weighted(p[...], j)

        def late_weights(p, j):
            p[:TILE] = jnp.exp2(scores(query[2, at(j)], j)).astype(jnp.bfloat16)

        def late_gather(p, j):
            acc[at(j)] += weighted(p[:TILE], j)

        def chunk(a, carry):
            first = 2 * a

            def turn(n, carry):
                j = 2 * n
                step(p1, j + 1, p0, j, first)
                step(p0, j + 2, p1, j + 1, first)
                return carry

            lax.fori_loop(0, a, turn, 0)
            late_weights(p1, first + 1)
            gather(p0, first, first)
            weights(p0, jnp.int32(0), jnp.minimum(first + 2, tiles - 2))
            late_gather(p1, first + 1)
            return carry

        weights(p0, jnp.int32(0), jnp.int32(0))
        lax.fori_loop(0, tiles // 2, chunk, 0)

    @pl.when(jnp.logical_not(fits))
    def _():
        lane = lax.broadcasted_iota(jnp.int32, (TILE, LANES), 1)

        def spread(x, n):
            return jnp.max(jnp.where(lane == n, x, -jnp.inf), axis=-1, keepdims=True)

        def row_block(i, carry):
            to = at(i)
            if final:
                x = acc[to]
                top[...] = jnp.where(own_fits, 0.0, spread(x, HEAD // 2)) + jnp.zeros_like(x)
                acc[to] = jnp.where(lane < HEAD, spread(x, 0), x)
            else:
                top[...] = jnp.full_like(top, LOW)

            def key_block(j, carry):
                s = scores(query[2 * (i == j).astype(jnp.int32), to], j)
                old = top[...]
                new = jnp.maximum(old, jnp.max(s, axis=-1, keepdims=True))
                p = jnp.exp2(s - jnp.concatenate([new] * (TILE // LANES), axis=1))
                acc[to] = acc[to] * jnp.exp2(old - new) + weighted(p.astype(jnp.bfloat16), j)
                top[...] = new
                return carry

            lax.fori_loop(0, i + 1, key_block, 0)
            if not final:
                x = acc[to]
                acc[to] = jnp.where((lane >= HEAD // 2) & (lane < HEAD), top[...], x)
            return carry

        lax.fori_loop(0, tiles, row_block, 0)

    if final:

        def finish(t, carry):
            base = pl.multiple_of(t * rows, rows)
            x = acc[pl.ds(base, half)]
            y = acc[pl.ds(base + half, half)]
            low = low_lanes(x.shape)
            num = jnp.where(low, swap(x), y)
            den = jnp.where(low, x, swap(y))
            out_ref[t] = (num / den).astype(jnp.bfloat16)
            return carry

        lax.fori_loop(0, HEADS, finish, 0, unroll=8)


def attend(*operands):
    rows = operands[0].shape[1] * 2 // 3
    final = len(operands) > 1
    total = HEADS * rows
    whole = pl.BlockSpec(memory_space=pltpu.VMEM)
    scalar = pl.BlockSpec(memory_space=pltpu.SMEM)
    far = pl.BlockSpec(memory_space=pl.ANY)
    bf16_rows = pltpu.VMEM((total, LANES), jnp.bfloat16)
    f32_rows = pltpu.VMEM((total, LANES), jnp.float32)
    scratch = [
        pltpu.VMEM((HEADS, rows // 2, LANES), jnp.bfloat16),
        pltpu.SemaphoreType.DMA((1,)),
        f32_rows,
    ] * final + [
        pltpu.VMEM((TILE, LANES), jnp.float32),
        pltpu.VMEM((3, total, LANES), jnp.bfloat16),
        bf16_rows,
        bf16_rows,
        pltpu.VMEM((CHUNK, TILE), jnp.bfloat16),
        pltpu.VMEM((CHUNK, TILE), jnp.bfloat16),
        pltpu.VMEM((rows // 2, LANES), jnp.float32),
        pltpu.VMEM((rows, LANES), jnp.float32),
    ]
    if final:
        out = jax.ShapeDtypeStruct((HEADS, rows // 2, LANES), jnp.bfloat16)
    else:
        out = [
            jax.ShapeDtypeStruct((total, LANES), jnp.float32),
            jax.ShapeDtypeStruct((1,), jnp.float32),
        ]
    pairs = total * total // 2
    return pl.pallas_call(
        functools.partial(attend_kernel, final),
        in_specs=[far, whole, whole, scalar] if final else [whole],
        out_specs=whole if final else [whole, scalar],
        out_shape=out,
        scratch_shapes=scratch,
        compiler_params=pltpu.CompilerParams(vmem_limit_bytes=20 << 20),
        cost_estimate=pl.CostEstimate(
            flops=16 * pairs * LANES, bytes_accessed=8 << 20, transcendentals=pairs
        ),
        name="attend_other" if final else "attend_own",
    )(*operands)


def out_kernel(a_ref, w_ref, o_ref, flat):
    half = a_ref.shape[1]

    for p in range(HEADS // 2):
        a = a_ref[2 * p].astype(jnp.float32)
        b = a_ref[2 * p + 1].astype(jnp.float32)
        low = low_lanes(a.shape)
        cols = slice(p * LANES, (p + 1) * LANES)
        flat[:half, cols] = jnp.where(low, a, swap(b)).astype(jnp.bfloat16)
        flat[half:, cols] = jnp.where(low, swap(a), b).astype(jnp.bfloat16)
    for c in range(0, w_ref.shape[1], COLS):
        mixed = jnp.dot(flat[...], w_ref[:, c : c + COLS], preferred_element_type=jnp.float32)
        mixed = [mixed[step * half : (step + 1) * half] for step in range(2)]
        o_ref[:, :, c : c + COLS] = jnp.stack(mixed, axis=1).astype(jnp.bfloat16)


def project_out(att, w_out):
    half = att.shape[1]
    width = w_out.shape[0]
    rows = 2 * half
    return pl.pallas_call(
        out_kernel,
        in_specs=[pl.BlockSpec(memory_space=pltpu.VMEM)] * 2,
        out_specs=pl.BlockSpec(memory_space=pltpu.VMEM),
        out_shape=jax.ShapeDtypeStruct((half, 2, width), jnp.bfloat16),
        scratch_shapes=[pltpu.VMEM((rows, width), jnp.bfloat16)],
        compiler_params=pltpu.CompilerParams(vmem_limit_bytes=24 << 20),
        cost_estimate=pl.CostEstimate(
            flops=2 * rows * width * width, bytes_accessed=2 * width * width, transcendentals=0
        ),
        name="project_out",
    )(att, w_out)


def block_for(adjacency, mine):
    blocks = jnp.arange(adjacency.shape[0], dtype=jnp.int32)
    row = lax.dynamic_index_in_dim(adjacency, mine, 0, keepdims=False)
    others = row * (blocks != mine).astype(jnp.int32)
    return jnp.sum(others * blocks) + (1 - jnp.sum(others)) * mine


def choose(index, options):
    return functools.reduce(
        lambda rest, at: jnp.where(index == at, options[at], rest),
        range(len(options) - 1),
        options[-1],
    )


def same_core(x):
    count = lax.axis_size("var")
    held = []
    for offset in range(1, count // 2):
        pairs = [(v, (v + 2 * offset) % count) for v in range(count)]
        held.append(lax.ppermute(x, "var", pairs))
    return held


def pick_other(held, adjacency):
    count = lax.axis_size("var")
    chips = count // 2
    mine = lax.axis_index("var")
    want = block_for(adjacency, mine)
    partner_want = block_for(adjacency, mine ^ 1)
    away = lambda block: (mine // 2 - block // 2 + chips) % chips
    to_send = choose(away(partner_want), held)
    got = lax.ppermute(to_send, "var", [(v, v ^ 1) for v in range(count)])
    slot = jnp.where(want % 2 == mine % 2, away(want), chips)
    return choose(slot, held + [got])


def local(tokens, gain, w_query, w_key, w_value, w_out, adjacency):
    gain = gain.reshape(1, -1)
    held = same_core(tokens)
    packed = project(tokens, gain, (w_key, w_value, w_query))
    *held, _ = lax.optimization_barrier((*held, packed))
    x_other = pick_other([tokens, *held], adjacency)
    kv_other = project(x_other, gain, (w_key, w_value))
    packed, _ = lax.optimization_barrier((exchange(packed), kv_other))
    kv_other = exchange(kv_other)
    att = exchange(attend(packed, kv_other, *attend(packed)))
    return project_out(att, w_out)


def solution(mesh):
    in_specs = (P("var", "tm", None), P(), P(), P(), P(), P(), P())
    out_specs = P("var", "tm", None)
    return jax.shard_map(local, mesh=mesh, in_specs=in_specs, out_specs=out_specs, check_vma=False)
```

```python
import functools
import math

import jax
import jax.numpy as jnp
from jax import lax
from jax.experimental import pallas as pl
from jax.experimental.pallas import tpu as pltpu
from jax.sharding import PartitionSpec as P

HEADS = 16
HEAD = 64
LANES = 2 * HEAD
COLS = 512
CHUNK = 1024
TILE = 512
LOW = -1e30
SAFE = 80.0


def exchange(x):
    return lax.all_to_all(x, "tm", split_axis=0, concat_axis=0, tiled=True)


def low_lanes(shape):
    return lax.broadcasted_iota(jnp.int32, shape, len(shape) - 1) < HEAD


def swap(x):
    return pltpu.roll(x, HEAD, x.ndim - 1)


def normed_rows(x_ref, gain_ref):
    x = x_ref[...].astype(jnp.float32)
    x = jnp.concatenate([x[:, step] for step in range(x.shape[1])], axis=0)
    meansq = jnp.mean(x * x, axis=-1, keepdims=True)
    return (x * lax.rsqrt(meansq + 1e-06) * gain_ref[...]).astype(jnp.bfloat16)


def project_kernel(with_query, *refs):
    x_ref, gain_ref, wk_ref, wv_ref = refs[:4]
    out_ref, normed_ref = refs[-2:]
    step = pl.program_id(0)

    @pl.when(step == 0)
    def _():
        normed_ref[...] = normed_rows(x_ref, gain_ref)

    normed = normed_ref[...]
    rows = normed.shape[0]
    half = rows // 2
    k = jnp.dot(normed, wk_ref[...], preferred_element_type=jnp.float32)
    v = jnp.dot(normed, wv_ref[...], preferred_element_type=jnp.float32)
    if with_query:
        q = jnp.dot(normed, refs[4][...], preferred_element_type=jnp.float32)
        q = q * (math.log2(math.e) / HEAD**0.5)
    for p in range(COLS // LANES):
        cols = slice(p * LANES, (p + 1) * LANES)
        kt, vt = k[:, cols], v[:, cols]
        low = low_lanes(kt.shape)
        out_ref[2 * p, :rows] = jnp.where(low, kt, swap(vt)).astype(jnp.bfloat16)
        out_ref[2 * p + 1, :rows] = jnp.where(low, swap(kt), vt).astype(jnp.bfloat16)
        if with_query:
            top, bottom = q[:half, cols], q[half:, cols]
            low = low_lanes(top.shape)
            out_ref[2 * p, rows:] = jnp.where(low, top, swap(bottom)).astype(jnp.bfloat16)
            out_ref[2 * p + 1, rows:] = jnp.where(low, swap(top), bottom).astype(jnp.bfloat16)


def project(x, gain, weights):
    var_rows, step_rows, width = x.shape
    rows = var_rows * step_rows
    with_query = len(weights) == 3
    out_rows = rows + rows // 2 if with_query else rows
    flops = 2 * rows * width * width * len(weights)
    return pl.pallas_call(
        functools.partial(project_kernel, with_query),
        grid=(width // COLS,),
        in_specs=[
            pl.BlockSpec(x.shape, lambda j: (0, 0, 0)),
            pl.BlockSpec((1, width), lambda j: (0, 0)),
        ]
        + [pl.BlockSpec((width, COLS), lambda j: (0, j))] * len(weights),
        out_specs=pl.BlockSpec((COLS // HEAD, out_rows, LANES), lambda j: (j, 0, 0)),
        out_shape=jax.ShapeDtypeStruct((HEADS, out_rows, LANES), jnp.bfloat16),
        scratch_shapes=[pltpu.VMEM((rows, width), jnp.bfloat16)],
        compiler_params=pltpu.CompilerParams(vmem_limit_bytes=(56 if with_query else 20) << 20),
        cost_estimate=pl.CostEstimate(
            flops=flops, bytes_accessed=2 * width * width * len(weights) + 4 * rows * width,
            transcendentals=0,
        ),
        name="project_own" if with_query else "project_other",
    )(x, gain, *weights)


def attend_kernel(final, *refs):
    q_ref, *refs = refs
    kv_ref = q_ref
    if final:
        q_far = q_ref
        kv_ref, state_in, longest_in, out_ref, q_ref, sem, acc, *refs = refs
        fetch = pltpu.make_async_copy(q_far.at[:, kv_ref.shape[1] :], q_ref, sem.at[0])
        fetch.start()
    else:
        acc, longest_out, *refs = refs
    top, query, key, value, p0, p1, query_len, key_len = refs
    rows = kv_ref.shape[1] if final else q_ref.shape[1] * 2 // 3
    half = rows // 2
    per = TILE // rows
    tiles = HEADS // per
    lane_of = lambda axis: lax.broadcasted_iota(jnp.int32, (LANES, LANES), axis) // HEAD
    same_half = (lane_of(0) == lane_of(1)).astype(jnp.bfloat16)
    key_half = (lane_of(0) == 0).astype(jnp.bfloat16)

    def lengths(x, ones):
        return jnp.dot((x * x).astype(jnp.bfloat16), ones, preferred_element_type=jnp.float32)

    def at(tile, count=1):
        return pl.ds(pl.multiple_of(tile * TILE, TILE), count * TILE)

    def prepare_queries(t, carry):
        x = q_ref[t, (0 if final else rows) :].astype(jnp.float32)
        if not final:
            query_len[...] = jnp.maximum(query_len[...], lengths(x, same_half))
        low = low_lanes(x.shape)
        lane = lax.broadcasted_iota(jnp.int32, x.shape, 1) - HEAD
        base = 2 * per * (t // per % 2)
        for part, y in enumerate((x, swap(x))):
            step = base + 2 * (t % per) + part
            later = jnp.where((lane > step) & (lane < base + 2 * per), LOW, jnp.float32(0.0))
            to = pl.ds(pl.multiple_of(t * rows + part * half, half), half)
            query[to] = jnp.where(low, y, later).astype(jnp.bfloat16)
        return carry

    def prepare(t, carry):
        block = pl.ds(pl.multiple_of(t * rows, rows), rows)
        kv = kv_ref[t, :rows].astype(jnp.float32)
        key_len[...] = jnp.maximum(key_len[...], lengths(kv, key_half))
        low = low_lanes(kv.shape)
        lane = lax.broadcasted_iota(jnp.int32, kv.shape, 1) - HEAD
        step = 2 * (t % (2 * per)) + lax.broadcasted_iota(jnp.int32, kv.shape, 0) // half
        is_step = jnp.where(lane == step, jnp.float32(1.0), jnp.float32(0.0))
        key[0, block] = jnp.where(low, kv, 0.0).astype(jnp.bfloat16)
        key[1, block] = jnp.where(low, kv, is_step).astype(jnp.bfloat16)
        value[block] = jnp.where(low, 1.0, kv).astype(jnp.bfloat16)
        acc[block] = state_in[block] if final else jnp.zeros((rows, LANES), jnp.float32)
        return carry

    query_len[...] = jnp.zeros_like(query_len)
    key_len[...] = jnp.zeros_like(key_len)
    if final:
        lax.fori_loop(0, HEADS, prepare, 0, unroll=8)
        fetch.wait()
        lax.fori_loop(0, HEADS, prepare_queries, 0, unroll=8)
    else:
        both = lambda t, carry: prepare(t, prepare_queries(t, carry))
        lax.fori_loop(0, HEADS, both, 0, unroll=8)
    longest = longest_in[0] if final else jnp.max(query_len[...])
    fits = longest * jnp.max(key_len[...]) <= SAFE * SAFE
    if final:
        own_fits = longest >= 0.0
        fits = fits & own_fits
    else:
        longest_out[0] = jnp.where(fits, longest, -1.0)

    def block_at(block, count=1):
        return pl.ds(pl.multiple_of(block * rows, rows), count * rows)

    def scores(q, k):
        return lax.dot_general(q, k, (((1,), (1,)), ((), ())), preferred_element_type=jnp.float32)

    def weighted(p, v):
        return jnp.dot(p, v, preferred_element_type=jnp.float32)

    @pl.when(fits)
    def _():
        def weights(p, j, first):
            p[...] = jnp.exp2(scores(query[at(first, 2)], key[0, at(j)])).astype(jnp.bfloat16)

        def gather(p, j, first):
            acc[at(first, 2)] += weighted(p[...], value[at(j)])

        def corner_weights(p, j, count):
            i = per * j
            s = scores(query[block_at(i)], key[1, block_at(i)])
            p[:rows, :rows] = jnp.exp2(s).astype(jnp.bfloat16)
            s = scores(query[block_at(i + 1, count - 1)], key[1, at(j)])
            p[rows : count * rows] = jnp.exp2(s).astype(jnp.bfloat16)

        def corner_gather(p, j, count):
            i = per * j
            acc[block_at(i)] += weighted(p[:rows, :rows], value[block_at(i)])
            acc[block_at(i + 1, count - 1)] += weighted(p[rows : count * rows], value[at(j)])

        def chunk(a, carry):
            first = 2 * a

            def turn(n, carry):
                j = 2 * n
                weights(p1, j + 1, first)
                gather(p0, j, first)
                weights(p0, j + 2, first)
                gather(p1, j + 1, first)
                return carry

            lax.fori_loop(0, a - 1, turn, 0)

            @pl.when(a > 0)
            def _():
                weights(p1, first - 1, first)
                gather(p0, first - 2, first)
                corner_weights(p0, first, 2 * per)
                gather(p1, first - 1, first)

            corner_weights(p1, first + 1, per)
            corner_gather(p0, first, 2 * per)
            weights(p0, jnp.int32(0), jnp.minimum(first + 2, tiles - 2))
            corner_gather(p1, first + 1, per)
            return carry

        corner_weights(p0, jnp.int32(0), 2 * per)
        lax.fori_loop(0, tiles // 2, chunk, 0)

    @pl.when(jnp.logical_not(fits))
    def _():
        lane = lax.broadcasted_iota(jnp.int32, (TILE, LANES), 1)

        def spread(x, n):
            return jnp.max(jnp.where(lane == n, x, -jnp.inf), axis=-1, keepdims=True)

        def row_block(i, carry):
            to = at(i)
            if final:
                x = acc[to]
                top[...] = jnp.where(own_fits, 0.0, spread(x, HEAD // 2)) + jnp.zeros_like(x)
                acc[to] = jnp.where(lane < HEAD, spread(x, 0), x)
            else:
                top[...] = jnp.full_like(top, LOW)

            def key_block(j, carry):
                s = scores(query[to], key[(i == j).astype(jnp.int32), at(j)])
                old = top[...]
                new = jnp.maximum(old, jnp.max(s, axis=-1, keepdims=True))
                p = jnp.exp2(s - jnp.concatenate([new] * (TILE // LANES), axis=1))
                acc[to] = acc[to] * jnp.exp2(old - new) + weighted(p.astype(jnp.bfloat16), value[at(j)])
                top[...] = new
                return carry

            lax.fori_loop(0, i + 1, key_block, 0)
            if not final:
                x = acc[to]
                acc[to] = jnp.where((lane >= HEAD // 2) & (lane < HEAD), top[...], x)
            return carry

        lax.fori_loop(0, tiles, row_block, 0)

    if final:

        def finish(t, carry):
            base = pl.multiple_of(t * rows, rows)
            x = acc[pl.ds(base, half)]
            y = acc[pl.ds(base + half, half)]
            low = low_lanes(x.shape)
            num = jnp.where(low, swap(x), y)
            den = jnp.where(low, x, swap(y))
            out_ref[t] = (num / den).astype(jnp.bfloat16)
            return carry

        lax.fori_loop(0, HEADS, finish, 0, unroll=8)


def attend(*operands):
    rows = operands[0].shape[1] * 2 // 3
    final = len(operands) > 1
    total = HEADS * rows
    whole = pl.BlockSpec(memory_space=pltpu.VMEM)
    scalar = pl.BlockSpec(memory_space=pltpu.SMEM)
    far = pl.BlockSpec(memory_space=pl.ANY)
    bf16_rows = pltpu.VMEM((total, LANES), jnp.bfloat16)
    f32_rows = pltpu.VMEM((total, LANES), jnp.float32)
    scratch = [
        pltpu.VMEM((HEADS, rows // 2, LANES), jnp.bfloat16),
        pltpu.SemaphoreType.DMA((1,)),
        f32_rows,
    ] * final + [
        pltpu.VMEM((TILE, LANES), jnp.float32),
        bf16_rows,
        pltpu.VMEM((2, total, LANES), jnp.bfloat16),
        bf16_rows,
        pltpu.VMEM((CHUNK, TILE), jnp.bfloat16),
        pltpu.VMEM((CHUNK, TILE), jnp.bfloat16),
        pltpu.VMEM((rows // 2, LANES), jnp.float32),
        pltpu.VMEM((rows, LANES), jnp.float32),
    ]
    if final:
        out = jax.ShapeDtypeStruct((HEADS, rows // 2, LANES), jnp.bfloat16)
    else:
        out = [
            jax.ShapeDtypeStruct((total, LANES), jnp.float32),
            jax.ShapeDtypeStruct((1,), jnp.float32),
        ]
    pairs = total * total // 2
    return pl.pallas_call(
        functools.partial(attend_kernel, final),
        in_specs=[far, whole, whole, scalar] if final else [whole],
        out_specs=whole if final else [whole, scalar],
        out_shape=out,
        scratch_shapes=scratch,
        compiler_params=pltpu.CompilerParams(vmem_limit_bytes=20 << 20),
        cost_estimate=pl.CostEstimate(
            flops=16 * pairs * LANES, bytes_accessed=8 << 20, transcendentals=pairs
        ),
        name="attend_other" if final else "attend_own",
    )(*operands)


def out_kernel(a_ref, w_ref, o_ref, flat):
    half = a_ref.shape[1]

    for p in range(HEADS // 2):
        a = a_ref[2 * p].astype(jnp.float32)
        b = a_ref[2 * p + 1].astype(jnp.float32)
        low = low_lanes(a.shape)
        cols = slice(p * LANES, (p + 1) * LANES)
        flat[:half, cols] = jnp.where(low, a, swap(b)).astype(jnp.bfloat16)
        flat[half:, cols] = jnp.where(low, swap(a), b).astype(jnp.bfloat16)
    for c in range(0, w_ref.shape[1], COLS):
        mixed = jnp.dot(flat[...], w_ref[:, c : c + COLS], preferred_element_type=jnp.float32)
        mixed = [mixed[step * half : (step + 1) * half] for step in range(2)]
        o_ref[:, :, c : c + COLS] = jnp.stack(mixed, axis=1).astype(jnp.bfloat16)


def project_out(att, w_out):
    half = att.shape[1]
    width = w_out.shape[0]
    rows = 2 * half
    return pl.pallas_call(
        out_kernel,
        in_specs=[pl.BlockSpec(memory_space=pltpu.VMEM)] * 2,
        out_specs=pl.BlockSpec(memory_space=pltpu.VMEM),
        out_shape=jax.ShapeDtypeStruct((half, 2, width), jnp.bfloat16),
        scratch_shapes=[pltpu.VMEM((rows, width), jnp.bfloat16)],
        compiler_params=pltpu.CompilerParams(vmem_limit_bytes=24 << 20),
        cost_estimate=pl.CostEstimate(
            flops=2 * rows * width * width, bytes_accessed=2 * width * width, transcendentals=0
        ),
        name="project_out",
    )(att, w_out)


def block_for(adjacency, mine):
    blocks = jnp.arange(adjacency.shape[0], dtype=jnp.int32)
    row = lax.dynamic_index_in_dim(adjacency, mine, 0, keepdims=False)
    others = row * (blocks != mine).astype(jnp.int32)
    return jnp.sum(others * blocks) + (1 - jnp.sum(others)) * mine


def choose(index, options):
    return functools.reduce(
        lambda rest, at: jnp.where(index == at, options[at], rest),
        range(len(options) - 1),
        options[-1],
    )


def same_core(x):
    count = lax.axis_size("var")
    held = []
    for offset in range(1, count // 2):
        pairs = [(v, (v + 2 * offset) % count) for v in range(count)]
        held.append(lax.ppermute(x, "var", pairs))
    return held


def pick_other(held, adjacency):
    count = lax.axis_size("var")
    chips = count // 2
    mine = lax.axis_index("var")
    want = block_for(adjacency, mine)
    partner_want = block_for(adjacency, mine ^ 1)
    away = lambda block: (mine // 2 - block // 2 + chips) % chips
    to_send = choose(away(partner_want), held)
    got = lax.ppermute(to_send, "var", [(v, v ^ 1) for v in range(count)])
    slot = jnp.where(want % 2 == mine % 2, away(want), chips)
    return choose(slot, held + [got])


def local(tokens, gain, w_query, w_key, w_value, w_out, adjacency):
    gain = gain.reshape(1, -1)
    held = same_core(tokens)
    packed = project(tokens, gain, (w_key, w_value, w_query))
    *held, _ = lax.optimization_barrier((*held, packed))
    x_other = pick_other([tokens, *held], adjacency)
    kv_other = project(x_other, gain, (w_key, w_value))
    packed, _ = lax.optimization_barrier((exchange(packed), kv_other))
    kv_other = exchange(kv_other)
    att = exchange(attend(packed, kv_other, *attend(packed)))
    return project_out(att, w_out)


def solution(mesh):
    in_specs = (P("var", "tm", None), P(), P(), P(), P(), P(), P())
    out_specs = P("var", "tm", None)
    return jax.shard_map(local, mesh=mesh, in_specs=in_specs, out_specs=out_specs, check_vma=False)
```

```python
import functools
import math

import jax
import jax.numpy as jnp
from jax import lax
from jax.experimental import pallas as pl
from jax.experimental.pallas import tpu as pltpu
from jax.sharding import PartitionSpec as P

HEADS = 16
HEAD = 64
LANES = 2 * HEAD
COLS = 512
CHUNK = 1024
TILE = 512
LOW = -1e30
SAFE = 80.0


def exchange(x):
    return lax.all_to_all(x, "tm", split_axis=0, concat_axis=0, tiled=True)


def low_lanes(shape):
    return lax.broadcasted_iota(jnp.int32, shape, len(shape) - 1) < HEAD


def swap(x):
    return pltpu.roll(x, HEAD, x.ndim - 1)


def normed_rows(x_ref, gain_ref):
    x = x_ref[...].astype(jnp.float32)
    x = jnp.concatenate([x[:, step] for step in range(x.shape[1])], axis=0)
    meansq = jnp.mean(x * x, axis=-1, keepdims=True)
    return (x * lax.rsqrt(meansq + 1e-06) * gain_ref[...]).astype(jnp.bfloat16)


def project_kernel(with_query, *refs):
    x_ref, gain_ref, wk_ref, wv_ref = refs[:4]
    out_ref, normed_ref = refs[-2:]
    step = pl.program_id(0)

    @pl.when(step == 0)
    def _():
        normed_ref[...] = normed_rows(x_ref, gain_ref)

    normed = normed_ref[...]
    rows = normed.shape[0]
    half = rows // 2
    k = jnp.dot(normed, wk_ref[...], preferred_element_type=jnp.float32)
    v = jnp.dot(normed, wv_ref[...], preferred_element_type=jnp.float32)
    if with_query:
        q = jnp.dot(normed, refs[4][...], preferred_element_type=jnp.float32)
        q = q * (math.log2(math.e) / HEAD**0.5)
    for p in range(COLS // LANES):
        cols = slice(p * LANES, (p + 1) * LANES)
        kt, vt = k[:, cols], v[:, cols]
        low = low_lanes(kt.shape)
        out_ref[2 * p, :rows] = jnp.where(low, kt, swap(vt)).astype(jnp.bfloat16)
        out_ref[2 * p + 1, :rows] = jnp.where(low, swap(kt), vt).astype(jnp.bfloat16)
        if with_query:
            top, bottom = q[:half, cols], q[half:, cols]
            low = low_lanes(top.shape)
            out_ref[2 * p, rows:] = jnp.where(low, top, swap(bottom)).astype(jnp.bfloat16)
            out_ref[2 * p + 1, rows:] = jnp.where(low, swap(top), bottom).astype(jnp.bfloat16)


def project(x, gain, weights):
    var_rows, step_rows, width = x.shape
    rows = var_rows * step_rows
    with_query = len(weights) == 3
    out_rows = rows + rows // 2 if with_query else rows
    flops = 2 * rows * width * width * len(weights)
    return pl.pallas_call(
        functools.partial(project_kernel, with_query),
        grid=(width // COLS,),
        in_specs=[
            pl.BlockSpec(x.shape, lambda j: (0, 0, 0)),
            pl.BlockSpec((1, width), lambda j: (0, 0)),
        ]
        + [pl.BlockSpec((width, COLS), lambda j: (0, j))] * len(weights),
        out_specs=pl.BlockSpec((COLS // HEAD, out_rows, LANES), lambda j: (j, 0, 0)),
        out_shape=jax.ShapeDtypeStruct((HEADS, out_rows, LANES), jnp.bfloat16),
        scratch_shapes=[pltpu.VMEM((rows, width), jnp.bfloat16)],
        compiler_params=pltpu.CompilerParams(vmem_limit_bytes=(56 if with_query else 20) << 20),
        cost_estimate=pl.CostEstimate(
            flops=flops, bytes_accessed=2 * width * width * len(weights) + 4 * rows * width,
            transcendentals=0,
        ),
        name="project_own" if with_query else "project_other",
    )(x, gain, *weights)


def attend_kernel(final, *refs):
    if final:
        kv_ref, query, state_in, longest_in, out_ref, acc, *refs = refs
        rows = kv_ref.shape[1]
    else:
        q_ref, acc, query, longest_out, *refs = refs
        kv_ref = q_ref
        rows = q_ref.shape[1] * 2 // 3
    top, key, value, p0, p1, query_len, key_len = refs
    half = rows // 2
    per = TILE // rows
    tiles = HEADS // per
    lane_of = lambda axis: lax.broadcasted_iota(jnp.int32, (LANES, LANES), axis) // HEAD
    same_half = (lane_of(0) == lane_of(1)).astype(jnp.bfloat16)
    key_half = (lane_of(0) == 0).astype(jnp.bfloat16)

    def lengths(x, ones):
        return jnp.dot((x * x).astype(jnp.bfloat16), ones, preferred_element_type=jnp.float32)

    def at(tile, count=1):
        return pl.ds(pl.multiple_of(tile * TILE, TILE), count * TILE)

    def prepare_queries(t, carry):
        x = q_ref[t, rows:].astype(jnp.float32)
        query_len[...] = jnp.maximum(query_len[...], lengths(x, same_half))
        low = low_lanes(x.shape)
        lane = lax.broadcasted_iota(jnp.int32, x.shape, 1) - HEAD
        base = 2 * per * (t // per % 2)
        for part, y in enumerate((x, swap(x))):
            step = base + 2 * (t % per) + part
            later = jnp.where((lane > step) & (lane < base + 2 * per), LOW, jnp.float32(0.0))
            to = pl.ds(pl.multiple_of(t * rows + part * half, half), half)
            query[to] = jnp.where(low, y, later).astype(jnp.bfloat16)
        return carry

    def prepare(t, carry):
        block = pl.ds(pl.multiple_of(t * rows, rows), rows)
        kv = kv_ref[t, :rows].astype(jnp.float32)
        key_len[...] = jnp.maximum(key_len[...], lengths(kv, key_half))
        low = low_lanes(kv.shape)
        lane = lax.broadcasted_iota(jnp.int32, kv.shape, 1) - HEAD
        step = 2 * (t % (2 * per)) + lax.broadcasted_iota(jnp.int32, kv.shape, 0) // half
        is_step = jnp.where(lane == step, jnp.float32(1.0), jnp.float32(0.0))
        key[0, block] = jnp.where(low, kv, 0.0).astype(jnp.bfloat16)
        key[1, block] = jnp.where(low, kv, is_step).astype(jnp.bfloat16)
        value[block] = jnp.where(low, 1.0, kv).astype(jnp.bfloat16)
        acc[block] = state_in[block] if final else jnp.zeros((rows, LANES), jnp.float32)
        return carry

    query_len[...] = jnp.zeros_like(query_len)
    key_len[...] = jnp.zeros_like(key_len)
    if final:
        lax.fori_loop(0, HEADS, prepare, 0, unroll=8)
    else:
        both = lambda t, carry: prepare(t, prepare_queries(t, carry))
        lax.fori_loop(0, HEADS, both, 0, unroll=8)
    longest = longest_in[0] if final else jnp.max(query_len[...])
    fits = longest * jnp.max(key_len[...]) <= SAFE * SAFE
    if final:
        own_fits = longest >= 0.0
        fits = fits & own_fits
    else:
        longest_out[0] = jnp.where(fits, longest, -1.0)

    def block_at(block, count=1):
        return pl.ds(pl.multiple_of(block * rows, rows), count * rows)

    def scores(q, k):
        return lax.dot_general(q, k, (((1,), (1,)), ((), ())), preferred_element_type=jnp.float32)

    def weighted(p, v):
        return jnp.dot(p, v, preferred_element_type=jnp.float32)

    @pl.when(fits)
    def _():
        def weights(p, j, first):
            p[...] = jnp.exp2(scores(query[at(first, 2)], key[0, at(j)])).astype(jnp.bfloat16)

        def gather(p, j, first):
            acc[at(first, 2)] += weighted(p[...], value[at(j)])

        def corner_weights(p, j, count):
            i = per * j
            s = scores(query[block_at(i)], key[1, block_at(i)])
            p[:rows, :rows] = jnp.exp2(s).astype(jnp.bfloat16)
            s = scores(query[block_at(i + 1, count - 1)], key[1, at(j)])
            p[rows : count * rows] = jnp.exp2(s).astype(jnp.bfloat16)

        def corner_gather(p, j, count):
            i = per * j
            acc[block_at(i)] += weighted(p[:rows, :rows], value[block_at(i)])
            acc[block_at(i + 1, count - 1)] += weighted(p[rows : count * rows], value[at(j)])

        def chunk(a, carry):
            first = 2 * a

            def turn(n, carry):
                j = 2 * n
                weights(p1, j + 1, first)
                gather(p0, j, first)
                weights(p0, j + 2, first)
                gather(p1, j + 1, first)
                return carry

            lax.fori_loop(0, a - 1, turn, 0)

            @pl.when(a > 0)
            def _():
                weights(p1, first - 1, first)
                gather(p0, first - 2, first)
                corner_weights(p0, first, 2 * per)
                gather(p1, first - 1, first)

            corner_weights(p1, first + 1, per)
            corner_gather(p0, first, 2 * per)
            weights(p0, jnp.int32(0), jnp.minimum(first + 2, tiles - 2))
            corner_gather(p1, first + 1, per)
            return carry

        corner_weights(p0, jnp.int32(0), 2 * per)
        lax.fori_loop(0, tiles // 2, chunk, 0)

    @pl.when(jnp.logical_not(fits))
    def _():
        lane = lax.broadcasted_iota(jnp.int32, (TILE, LANES), 1)

        def spread(x, n):
            return jnp.max(jnp.where(lane == n, x, -jnp.inf), axis=-1, keepdims=True)

        def row_block(i, carry):
            to = at(i)
            if final:
                x = acc[to]
                top[...] = jnp.where(own_fits, 0.0, spread(x, HEAD // 2)) + jnp.zeros_like(x)
                acc[to] = jnp.where(lane < HEAD, spread(x, 0), x)
            else:
                top[...] = jnp.full_like(top, LOW)

            def key_block(j, carry):
                s = scores(query[to], key[(i == j).astype(jnp.int32), at(j)])
                old = top[...]
                new = jnp.maximum(old, jnp.max(s, axis=-1, keepdims=True))
                p = jnp.exp2(s - jnp.concatenate([new] * (TILE // LANES), axis=1))
                acc[to] = acc[to] * jnp.exp2(old - new) + weighted(p.astype(jnp.bfloat16), value[at(j)])
                top[...] = new
                return carry

            lax.fori_loop(0, i + 1, key_block, 0)
            if not final:
                x = acc[to]
                acc[to] = jnp.where((lane >= HEAD // 2) & (lane < HEAD), top[...], x)
            return carry

        lax.fori_loop(0, tiles, row_block, 0)

    if final:

        def finish(t, carry):
            base = pl.multiple_of(t * rows, rows)
            x = acc[pl.ds(base, half)]
            y = acc[pl.ds(base + half, half)]
            low = low_lanes(x.shape)
            num = jnp.where(low, swap(x), y)
            den = jnp.where(low, x, swap(y))
            out_ref[t] = (num / den).astype(jnp.bfloat16)
            return carry

        lax.fori_loop(0, HEADS, finish, 0, unroll=8)


def attend(*operands):
    final = len(operands) > 1
    rows = operands[0].shape[1] if final else operands[0].shape[1] * 2 // 3
    total = HEADS * rows
    whole = pl.BlockSpec(memory_space=pltpu.VMEM)
    scalar = pl.BlockSpec(memory_space=pltpu.SMEM)
    bf16_rows = pltpu.VMEM((total, LANES), jnp.bfloat16)
    f32_rows = pltpu.VMEM((total, LANES), jnp.float32)
    scratch = [f32_rows] * final + [
        pltpu.VMEM((TILE, LANES), jnp.float32),
        pltpu.VMEM((2, total, LANES), jnp.bfloat16),
        bf16_rows,
        pltpu.VMEM((CHUNK, TILE), jnp.bfloat16),
        pltpu.VMEM((CHUNK, TILE), jnp.bfloat16),
        pltpu.VMEM((rows // 2, LANES), jnp.float32),
        pltpu.VMEM((rows, LANES), jnp.float32),
    ]
    if final:
        out = jax.ShapeDtypeStruct((HEADS, rows // 2, LANES), jnp.bfloat16)
    else:
        out = [
            jax.ShapeDtypeStruct((total, LANES), jnp.float32),
            jax.ShapeDtypeStruct((total, LANES), jnp.bfloat16),
            jax.ShapeDtypeStruct((1,), jnp.float32),
        ]
    pairs = total * total // 2
    return pl.pallas_call(
        functools.partial(attend_kernel, final),
        in_specs=[whole, whole, whole, scalar] if final else [whole],
        out_specs=whole if final else [whole, whole, scalar],
        out_shape=out,
        scratch_shapes=scratch,
        compiler_params=pltpu.CompilerParams(vmem_limit_bytes=20 << 20),
        cost_estimate=pl.CostEstimate(
            flops=16 * pairs * LANES, bytes_accessed=8 << 20, transcendentals=pairs
        ),
        name="attend_other" if final else "attend_own",
    )(*operands)


def out_kernel(a_ref, w_ref, o_ref, flat):
    half = a_ref.shape[1]

    for p in range(HEADS // 2):
        a = a_ref[2 * p].astype(jnp.float32)
        b = a_ref[2 * p + 1].astype(jnp.float32)
        low = low_lanes(a.shape)
        cols = slice(p * LANES, (p + 1) * LANES)
        flat[:half, cols] = jnp.where(low, a, swap(b)).astype(jnp.bfloat16)
        flat[half:, cols] = jnp.where(low, swap(a), b).astype(jnp.bfloat16)
    for c in range(0, w_ref.shape[1], COLS):
        mixed = jnp.dot(flat[...], w_ref[:, c : c + COLS], preferred_element_type=jnp.float32)
        mixed = [mixed[step * half : (step + 1) * half] for step in range(2)]
        o_ref[:, :, c : c + COLS] = jnp.stack(mixed, axis=1).astype(jnp.bfloat16)


def project_out(att, w_out):
    half = att.shape[1]
    width = w_out.shape[0]
    rows = 2 * half
    return pl.pallas_call(
        out_kernel,
        in_specs=[pl.BlockSpec(memory_space=pltpu.VMEM)] * 2,
        out_specs=pl.BlockSpec(memory_space=pltpu.VMEM),
        out_shape=jax.ShapeDtypeStruct((half, 2, width), jnp.bfloat16),
        scratch_shapes=[pltpu.VMEM((rows, width), jnp.bfloat16)],
        compiler_params=pltpu.CompilerParams(vmem_limit_bytes=24 << 20),
        cost_estimate=pl.CostEstimate(
            flops=2 * rows * width * width, bytes_accessed=2 * width * width, transcendentals=0
        ),
        name="project_out",
    )(att, w_out)


def block_for(adjacency, mine):
    blocks = jnp.arange(adjacency.shape[0], dtype=jnp.int32)
    row = lax.dynamic_index_in_dim(adjacency, mine, 0, keepdims=False)
    others = row * (blocks != mine).astype(jnp.int32)
    return jnp.sum(others * blocks) + (1 - jnp.sum(others)) * mine


def choose(index, options):
    return functools.reduce(
        lambda rest, at: jnp.where(index == at, options[at], rest),
        range(len(options) - 1),
        options[-1],
    )


def same_core(x):
    count = lax.axis_size("var")
    held = []
    for offset in range(1, count // 2):
        pairs = [(v, (v + 2 * offset) % count) for v in range(count)]
        held.append(lax.ppermute(x, "var", pairs))
    return held


def pick_other(held, adjacency):
    count = lax.axis_size("var")
    chips = count // 2
    mine = lax.axis_index("var")
    want = block_for(adjacency, mine)
    partner_want = block_for(adjacency, mine ^ 1)
    away = lambda block: (mine // 2 - block // 2 + chips) % chips
    to_send = choose(away(partner_want), held)
    got = lax.ppermute(to_send, "var", [(v, v ^ 1) for v in range(count)])
    slot = jnp.where(want % 2 == mine % 2, away(want), chips)
    return choose(slot, held + [got])


def local(tokens, gain, w_query, w_key, w_value, w_out, adjacency):
    gain = gain.reshape(1, -1)
    held = same_core(tokens)
    packed = project(tokens, gain, (w_key, w_value, w_query))
    *held, _ = lax.optimization_barrier((*held, packed))
    x_other = pick_other([tokens, *held], adjacency)
    kv_other = project(x_other, gain, (w_key, w_value))
    packed, _ = lax.optimization_barrier((exchange(packed), kv_other))
    kv_other = exchange(kv_other)
    state, query, longest = attend(packed)
    att = exchange(attend(kv_other, query, state, longest))
    return project_out(att, w_out)


def solution(mesh):
    in_specs = (P("var", "tm", None), P(), P(), P(), P(), P(), P())
    out_specs = P("var", "tm", None)
    return jax.shard_map(local, mesh=mesh, in_specs=in_specs, out_specs=out_specs, check_vma=False)
```

```python
import functools
import math

import jax
import jax.numpy as jnp
from jax import lax
from jax.experimental import pallas as pl
from jax.experimental.pallas import tpu as pltpu
from jax.sharding import PartitionSpec as P

HEADS = 16
HEAD = 64
LANES = 2 * HEAD
COLS = 512
CHUNK = 1024
TILE = 512
LOW = -1e30
SAFE = 80.0


def exchange(x):
    return lax.all_to_all(x, "tm", split_axis=0, concat_axis=0, tiled=True)


def low_lanes(shape):
    return lax.broadcasted_iota(jnp.int32, shape, len(shape) - 1) < HEAD


def swap(x):
    return pltpu.roll(x, HEAD, x.ndim - 1)


def normed_rows(x_ref, gain_ref):
    x = x_ref[...].astype(jnp.float32)
    x = jnp.concatenate([x[:, step] for step in range(x.shape[1])], axis=0)
    meansq = jnp.mean(x * x, axis=-1, keepdims=True)
    return (x * lax.rsqrt(meansq + 1e-06) * gain_ref[...]).astype(jnp.bfloat16)


def project_kernel(with_query, *refs):
    x_ref, gain_ref, wk_ref, wv_ref = refs[:4]
    out_ref, normed_ref = refs[-2:]
    step = pl.program_id(0)

    @pl.when(step == 0)
    def _():
        normed_ref[...] = normed_rows(x_ref, gain_ref)

    normed = normed_ref[...]
    rows = normed.shape[0]
    half = rows // 2
    k = jnp.dot(normed, wk_ref[...], preferred_element_type=jnp.float32)
    v = jnp.dot(normed, wv_ref[...], preferred_element_type=jnp.float32)
    if with_query:
        q = jnp.dot(normed, refs[4][...], preferred_element_type=jnp.float32)
        q = q * (math.log2(math.e) / HEAD**0.5)
    for p in range(COLS // LANES):
        cols = slice(p * LANES, (p + 1) * LANES)
        kt, vt = k[:, cols], v[:, cols]
        low = low_lanes(kt.shape)
        out_ref[2 * p, :rows] = jnp.where(low, kt, swap(vt)).astype(jnp.bfloat16)
        out_ref[2 * p + 1, :rows] = jnp.where(low, swap(kt), vt).astype(jnp.bfloat16)
        if with_query:
            top, bottom = q[:half, cols], q[half:, cols]
            low = low_lanes(top.shape)
            out_ref[2 * p, rows:] = jnp.where(low, top, swap(bottom)).astype(jnp.bfloat16)
            out_ref[2 * p + 1, rows:] = jnp.where(low, swap(top), bottom).astype(jnp.bfloat16)


def project(x, gain, weights):
    var_rows, step_rows, width = x.shape
    rows = var_rows * step_rows
    with_query = len(weights) == 3
    out_rows = rows + rows // 2 if with_query else rows
    flops = 2 * rows * width * width * len(weights)
    return pl.pallas_call(
        functools.partial(project_kernel, with_query),
        grid=(width // COLS,),
        in_specs=[
            pl.BlockSpec(x.shape, lambda j: (0, 0, 0)),
            pl.BlockSpec((1, width), lambda j: (0, 0)),
        ]
        + [pl.BlockSpec((width, COLS), lambda j: (0, j))] * len(weights),
        out_specs=pl.BlockSpec((COLS // HEAD, out_rows, LANES), lambda j: (j, 0, 0)),
        out_shape=jax.ShapeDtypeStruct((HEADS, out_rows, LANES), jnp.bfloat16),
        scratch_shapes=[pltpu.VMEM((rows, width), jnp.bfloat16)],
        compiler_params=pltpu.CompilerParams(vmem_limit_bytes=(56 if with_query else 20) << 20),
        cost_estimate=pl.CostEstimate(
            flops=flops, bytes_accessed=2 * width * width * len(weights) + 4 * rows * width,
            transcendentals=0,
        ),
        name="project_own" if with_query else "project_other",
    )(x, gain, *weights)


def attend_kernel(final, *refs):
    q_ref, *refs = refs
    kv_ref = q_ref
    if final:
        q_far = q_ref
        kv_ref, state_in, longest_in, out_ref, q_ref, sem, acc, *refs = refs
        fetch = pltpu.make_async_copy(q_far.at[:, kv_ref.shape[1] :], q_ref, sem.at[0])
        fetch.start()
    else:
        acc, longest_out, *refs = refs
    top, query, key, value, p0, p1, query_len, key_len = refs
    rows = kv_ref.shape[1] if final else q_ref.shape[1] * 2 // 3
    half = rows // 2
    per = TILE // rows
    tiles = HEADS // per
    lane_of = lambda axis: lax.broadcasted_iota(jnp.int32, (LANES, LANES), axis) // HEAD
    same_half = (lane_of(0) == lane_of(1)).astype(jnp.bfloat16)
    key_half = (lane_of(0) == 0).astype(jnp.bfloat16)

    def lengths(x, ones):
        return jnp.dot((x * x).astype(jnp.bfloat16), ones, preferred_element_type=jnp.float32)

    def at(tile, count=1):
        return pl.ds(pl.multiple_of(tile * TILE, TILE), count * TILE)

    def prepare_queries(t, carry):
        x = q_ref[t, (0 if final else rows) :].astype(jnp.float32)
        if not final:
            query_len[...] = jnp.maximum(query_len[...], lengths(x, same_half))
        low = low_lanes(x.shape)
        lane = lax.broadcasted_iota(jnp.int32, x.shape, 1) - HEAD
        base = 2 * per * (t // per % 2)
        for part, y in enumerate((x, swap(x))):
            step = base + 2 * (t % per) + part
            later = jnp.where((lane > step) & (lane < base + 2 * per), LOW, jnp.float32(0.0))
            to = pl.ds(pl.multiple_of(t * rows + part * half, half), half)
            query[to] = jnp.where(low, y, later).astype(jnp.bfloat16)
        return carry

    def prepare(t, carry):
        block = pl.ds(pl.multiple_of(t * rows, rows), rows)
        kv = kv_ref[t, :rows].astype(jnp.float32)
        key_len[...] = jnp.maximum(key_len[...], lengths(kv, key_half))
        low = low_lanes(kv.shape)
        lane = lax.broadcasted_iota(jnp.int32, kv.shape, 1) - HEAD
        step = 2 * (t % (2 * per)) + lax.broadcasted_iota(jnp.int32, kv.shape, 0) // half
        is_step = jnp.where(lane == step, jnp.float32(1.0), jnp.float32(0.0))
        key[0, block] = jnp.where(low, kv, 0.0).astype(jnp.bfloat16)
        key[1, block] = jnp.where(low, kv, is_step).astype(jnp.bfloat16)
        value[block] = jnp.where(low, 1.0, kv).astype(jnp.bfloat16)
        acc[block] = state_in[block] if final else jnp.zeros((rows, LANES), jnp.float32)
        return carry

    query_len[...] = jnp.zeros_like(query_len)
    key_len[...] = jnp.zeros_like(key_len)
    if final:
        lax.fori_loop(0, HEADS, prepare, 0, unroll=8)
        fetch.wait()
        lax.fori_loop(0, HEADS, prepare_queries, 0, unroll=8)
    else:
        both = lambda t, carry: prepare(t, prepare_queries(t, carry))
        lax.fori_loop(0, HEADS, both, 0, unroll=8)
    longest = longest_in[0] if final else jnp.max(query_len[...])
    fits = longest * jnp.max(key_len[...]) <= SAFE * SAFE
    if final:
        own_fits = longest >= 0.0
        fits = fits & own_fits
    else:
        longest_out[0] = jnp.where(fits, longest, -1.0)

    def block_at(block, count=1):
        return pl.ds(pl.multiple_of(block * rows, rows), count * rows)

    def scores(q, k):
        return lax.dot_general(q, k, (((1,), (1,)), ((), ())), preferred_element_type=jnp.float32)

    def weighted(p, v):
        return jnp.dot(p, v, preferred_element_type=jnp.float32)

    @pl.when(fits)
    def _():
        def spans(first, j):
            start, diagonal = first * per, j >= first
            if not diagonal:
                return [(0, start, 2 * per, j * per, per)]
            corner = j * per
            return [
                (0, corner, 1, corner, 1),
                (1, corner + 1, start + 2 * per - corner - 1, corner, per),
            ]

        def weights(p, first, j):
            version = int(j >= first)
            for at_row, row, count, column, width in spans(first, j):
                s = scores(query[block_at(row, count)], key[version, block_at(column, width)])
                here = slice(at_row * rows, (at_row + count) * rows)
                p[here, : width * rows] = jnp.exp2(s).astype(jnp.bfloat16)

        def gather(p, first, j):
            for at_row, row, count, column, width in spans(first, j):
                here = slice(at_row * rows, (at_row + count) * rows)
                v = value[block_at(column, width)]
                acc[block_at(row, count)] += weighted(p[here, : width * rows], v)

        todo = [(first, j) for first in range(0, tiles, 2) for j in range(first + 2)]
        slots = (p0, p1)
        weights(p0, *todo[0])
        for n, here in enumerate(todo):
            if n + 1 < len(todo):
                weights(slots[(n + 1) % 2], *todo[n + 1])
            gather(slots[n % 2], *here)

    @pl.when(jnp.logical_not(fits))
    def _():
        lane = lax.broadcasted_iota(jnp.int32, (TILE, LANES), 1)

        def spread(x, n):
            return jnp.max(jnp.where(lane == n, x, -jnp.inf), axis=-1, keepdims=True)

        def row_block(i, carry):
            to = at(i)
            if final:
                x = acc[to]
                top[...] = jnp.where(own_fits, 0.0, spread(x, HEAD // 2)) + jnp.zeros_like(x)
                acc[to] = jnp.where(lane < HEAD, spread(x, 0), x)
            else:
                top[...] = jnp.full_like(top, LOW)

            def key_block(j, carry):
                s = scores(query[to], key[(i == j).astype(jnp.int32), at(j)])
                old = top[...]
                new = jnp.maximum(old, jnp.max(s, axis=-1, keepdims=True))
                p = jnp.exp2(s - jnp.concatenate([new] * (TILE // LANES), axis=1))
                acc[to] = acc[to] * jnp.exp2(old - new) + weighted(p.astype(jnp.bfloat16), value[at(j)])
                top[...] = new
                return carry

            lax.fori_loop(0, i + 1, key_block, 0)
            if not final:
                x = acc[to]
                acc[to] = jnp.where((lane >= HEAD // 2) & (lane < HEAD), top[...], x)
            return carry

        lax.fori_loop(0, tiles, row_block, 0)

    if final:

        def finish(t, carry):
            base = pl.multiple_of(t * rows, rows)
            x = acc[pl.ds(base, half)]
            y = acc[pl.ds(base + half, half)]
            low = low_lanes(x.shape)
            num = jnp.where(low, swap(x), y)
            den = jnp.where(low, x, swap(y))
            out_ref[t] = (num / den).astype(jnp.bfloat16)
            return carry

        lax.fori_loop(0, HEADS, finish, 0, unroll=8)


def attend(*operands):
    rows = operands[0].shape[1] * 2 // 3
    final = len(operands) > 1
    total = HEADS * rows
    whole = pl.BlockSpec(memory_space=pltpu.VMEM)
    scalar = pl.BlockSpec(memory_space=pltpu.SMEM)
    far = pl.BlockSpec(memory_space=pl.ANY)
    bf16_rows = pltpu.VMEM((total, LANES), jnp.bfloat16)
    f32_rows = pltpu.VMEM((total, LANES), jnp.float32)
    scratch = [
        pltpu.VMEM((HEADS, rows // 2, LANES), jnp.bfloat16),
        pltpu.SemaphoreType.DMA((1,)),
        f32_rows,
    ] * final + [
        pltpu.VMEM((TILE, LANES), jnp.float32),
        bf16_rows,
        pltpu.VMEM((2, total, LANES), jnp.bfloat16),
        bf16_rows,
        pltpu.VMEM((CHUNK, TILE), jnp.bfloat16),
        pltpu.VMEM((CHUNK, TILE), jnp.bfloat16),
        pltpu.VMEM((rows // 2, LANES), jnp.float32),
        pltpu.VMEM((rows, LANES), jnp.float32),
    ]
    if final:
        out = jax.ShapeDtypeStruct((HEADS, rows // 2, LANES), jnp.bfloat16)
    else:
        out = [
            jax.ShapeDtypeStruct((total, LANES), jnp.float32),
            jax.ShapeDtypeStruct((1,), jnp.float32),
        ]
    pairs = total * total // 2
    return pl.pallas_call(
        functools.partial(attend_kernel, final),
        in_specs=[far, whole, whole, scalar] if final else [whole],
        out_specs=whole if final else [whole, scalar],
        out_shape=out,
        scratch_shapes=scratch,
        compiler_params=pltpu.CompilerParams(vmem_limit_bytes=20 << 20),
        cost_estimate=pl.CostEstimate(
            flops=16 * pairs * LANES, bytes_accessed=8 << 20, transcendentals=pairs
        ),
        name="attend_other" if final else "attend_own",
    )(*operands)


def out_kernel(a_ref, w_ref, o_ref, flat):
    half = a_ref.shape[1]

    for p in range(HEADS // 2):
        a = a_ref[2 * p].astype(jnp.float32)
        b = a_ref[2 * p + 1].astype(jnp.float32)
        low = low_lanes(a.shape)
        cols = slice(p * LANES, (p + 1) * LANES)
        flat[:half, cols] = jnp.where(low, a, swap(b)).astype(jnp.bfloat16)
        flat[half:, cols] = jnp.where(low, swap(a), b).astype(jnp.bfloat16)
    for c in range(0, w_ref.shape[1], COLS):
        mixed = jnp.dot(flat[...], w_ref[:, c : c + COLS], preferred_element_type=jnp.float32)
        mixed = [mixed[step * half : (step + 1) * half] for step in range(2)]
        o_ref[:, :, c : c + COLS] = jnp.stack(mixed, axis=1).astype(jnp.bfloat16)


def project_out(att, w_out):
    half = att.shape[1]
    width = w_out.shape[0]
    rows = 2 * half
    return pl.pallas_call(
        out_kernel,
        in_specs=[pl.BlockSpec(memory_space=pltpu.VMEM)] * 2,
        out_specs=pl.BlockSpec(memory_space=pltpu.VMEM),
        out_shape=jax.ShapeDtypeStruct((half, 2, width), jnp.bfloat16),
        scratch_shapes=[pltpu.VMEM((rows, width), jnp.bfloat16)],
        compiler_params=pltpu.CompilerParams(vmem_limit_bytes=24 << 20),
        cost_estimate=pl.CostEstimate(
            flops=2 * rows * width * width, bytes_accessed=2 * width * width, transcendentals=0
        ),
        name="project_out",
    )(att, w_out)


def block_for(adjacency, mine):
    blocks = jnp.arange(adjacency.shape[0], dtype=jnp.int32)
    row = lax.dynamic_index_in_dim(adjacency, mine, 0, keepdims=False)
    others = row * (blocks != mine).astype(jnp.int32)
    return jnp.sum(others * blocks) + (1 - jnp.sum(others)) * mine


def choose(index, options):
    return functools.reduce(
        lambda rest, at: jnp.where(index == at, options[at], rest),
        range(len(options) - 1),
        options[-1],
    )


def same_core(x):
    count = lax.axis_size("var")
    held = []
    for offset in range(1, count // 2):
        pairs = [(v, (v + 2 * offset) % count) for v in range(count)]
        held.append(lax.ppermute(x, "var", pairs))
    return held


def pick_other(held, adjacency):
    count = lax.axis_size("var")
    chips = count // 2
    mine = lax.axis_index("var")
    want = block_for(adjacency, mine)
    partner_want = block_for(adjacency, mine ^ 1)
    away = lambda block: (mine // 2 - block // 2 + chips) % chips
    to_send = choose(away(partner_want), held)
    got = lax.ppermute(to_send, "var", [(v, v ^ 1) for v in range(count)])
    slot = jnp.where(want % 2 == mine % 2, away(want), chips)
    return choose(slot, held + [got])


def local(tokens, gain, w_query, w_key, w_value, w_out, adjacency):
    gain = gain.reshape(1, -1)
    held = same_core(tokens)
    packed = project(tokens, gain, (w_key, w_value, w_query))
    *held, _ = lax.optimization_barrier((*held, packed))
    x_other = pick_other([tokens, *held], adjacency)
    kv_other = project(x_other, gain, (w_key, w_value))
    packed, _ = lax.optimization_barrier((exchange(packed), kv_other))
    kv_other = exchange(kv_other)
    att = exchange(attend(packed, kv_other, *attend(packed)))
    return project_out(att, w_out)


def solution(mesh):
    in_specs = (P("var", "tm", None), P(), P(), P(), P(), P(), P())
    out_specs = P("var", "tm", None)
    return jax.shard_map(local, mesh=mesh, in_specs=in_specs, out_specs=out_specs, check_vma=False)
```

```python
import functools
import math

import jax
import jax.numpy as jnp
from jax import lax
from jax.experimental import pallas as pl
from jax.experimental.pallas import tpu as pltpu
from jax.sharding import PartitionSpec as P

HEADS = 16
HEAD = 64
LANES = 2 * HEAD
COLS = 512
CHUNK = 1024
TILE = 512
LOW = -1e30
SAFE = 80.0


def exchange(x):
    return lax.all_to_all(x, "tm", split_axis=0, concat_axis=0, tiled=True)


def low_lanes(shape):
    return lax.broadcasted_iota(jnp.int32, shape, len(shape) - 1) < HEAD


def swap(x):
    return pltpu.roll(x, HEAD, x.ndim - 1)


def normed_rows(x_ref, gain_ref):
    x = x_ref[...].astype(jnp.float32)
    x = jnp.concatenate([x[:, step] for step in range(x.shape[1])], axis=0)
    meansq = jnp.mean(x * x, axis=-1, keepdims=True)
    return (x * lax.rsqrt(meansq + 1e-06) * gain_ref[...]).astype(jnp.bfloat16)


def project_kernel(with_query, *refs):
    x_ref, gain_ref, wk_ref, wv_ref = refs[:4]
    out_ref, normed_ref = refs[-2:]
    step = pl.program_id(0)

    @pl.when(step == 0)
    def _():
        normed_ref[...] = normed_rows(x_ref, gain_ref)

    normed = normed_ref[...]
    rows = normed.shape[0]
    half = rows // 2
    k = jnp.dot(normed, wk_ref[...], preferred_element_type=jnp.float32)
    v = jnp.dot(normed, wv_ref[...], preferred_element_type=jnp.float32)
    if with_query:
        q = jnp.dot(normed, refs[4][...], preferred_element_type=jnp.float32)
        q = q * (math.log2(math.e) / HEAD**0.5)
    for p in range(COLS // LANES):
        cols = slice(p * LANES, (p + 1) * LANES)
        kt, vt = k[:, cols], v[:, cols]
        low = low_lanes(kt.shape)
        out_ref[2 * p, :rows] = jnp.where(low, kt, swap(vt)).astype(jnp.bfloat16)
        out_ref[2 * p + 1, :rows] = jnp.where(low, swap(kt), vt).astype(jnp.bfloat16)
        if with_query:
            top, bottom = q[:half, cols], q[half:, cols]
            low = low_lanes(top.shape)
            out_ref[2 * p, rows:] = jnp.where(low, top, swap(bottom)).astype(jnp.bfloat16)
            out_ref[2 * p + 1, rows:] = jnp.where(low, swap(top), bottom).astype(jnp.bfloat16)


def project(x, gain, weights):
    var_rows, step_rows, width = x.shape
    rows = var_rows * step_rows
    with_query = len(weights) == 3
    out_rows = rows + rows // 2 if with_query else rows
    flops = 2 * rows * width * width * len(weights)
    return pl.pallas_call(
        functools.partial(project_kernel, with_query),
        grid=(width // COLS,),
        in_specs=[
            pl.BlockSpec(x.shape, lambda j: (0, 0, 0)),
            pl.BlockSpec((1, width), lambda j: (0, 0)),
        ]
        + [pl.BlockSpec((width, COLS), lambda j: (0, j))] * len(weights),
        out_specs=pl.BlockSpec((COLS // HEAD, out_rows, LANES), lambda j: (j, 0, 0)),
        out_shape=jax.ShapeDtypeStruct((HEADS, out_rows, LANES), jnp.bfloat16),
        scratch_shapes=[pltpu.VMEM((rows, width), jnp.bfloat16)],
        compiler_params=pltpu.CompilerParams(vmem_limit_bytes=(56 if with_query else 20) << 20),
        cost_estimate=pl.CostEstimate(
            flops=flops, bytes_accessed=2 * width * width * len(weights) + 4 * rows * width,
            transcendentals=0,
        ),
        name="project_own" if with_query else "project_other",
    )(x, gain, *weights)


def attend_kernel(final, *refs):
    q_ref, *refs = refs
    kv_ref = q_ref
    if final:
        q_far = q_ref
        kv_ref, state_in, longest_in, out_ref, q_ref, sem, acc, *refs = refs
        fetch = pltpu.make_async_copy(q_far.at[:, kv_ref.shape[1] :], q_ref, sem.at[0])
        fetch.start()
    else:
        acc, longest_out, *refs = refs
    top, query, key, value, p0, p1, query_len, key_len = refs
    rows = kv_ref.shape[1] if final else q_ref.shape[1] * 2 // 3
    half = rows // 2
    per = TILE // rows
    tiles = HEADS // per
    lane_of = lambda axis: lax.broadcasted_iota(jnp.int32, (LANES, LANES), axis) // HEAD
    same_half = (lane_of(0) == lane_of(1)).astype(jnp.bfloat16)
    key_half = (lane_of(0) == 0).astype(jnp.bfloat16)

    def lengths(x, ones):
        return jnp.dot((x * x).astype(jnp.bfloat16), ones, preferred_element_type=jnp.float32)

    def at(tile, count=1):
        return pl.ds(pl.multiple_of(tile * TILE, TILE), count * TILE)

    def prepare_queries(t):
        x = q_ref[t, (0 if final else rows) :].astype(jnp.float32)
        if not final:
            query_len[...] = jnp.maximum(query_len[...], lengths(x, same_half))
        low = low_lanes(x.shape)
        lane = lax.broadcasted_iota(jnp.int32, x.shape, 1) - HEAD
        base = 2 * per * (t // per % 2)
        for part, y in enumerate((x, swap(x))):
            step = base + 2 * (t % per) + part
            later = jnp.where((lane > step) & (lane < base + 2 * per), LOW, jnp.float32(0.0))
            to = pl.ds(pl.multiple_of(t * rows + part * half, half), half)
            query[to] = jnp.where(low, y, later).astype(jnp.bfloat16)

    def prepare(t):
        block = pl.ds(pl.multiple_of(t * rows, rows), rows)
        kv = kv_ref[t, :rows].astype(jnp.float32)
        key_len[...] = jnp.maximum(key_len[...], lengths(kv, key_half))
        low = low_lanes(kv.shape)
        lane = lax.broadcasted_iota(jnp.int32, kv.shape, 1) - HEAD
        step = 2 * (t % (2 * per)) + lax.broadcasted_iota(jnp.int32, kv.shape, 0) // half
        is_step = jnp.where(lane == step, jnp.float32(1.0), jnp.float32(0.0))
        key[0, block] = jnp.where(low, kv, 0.0).astype(jnp.bfloat16)
        key[1, block] = jnp.where(low, kv, is_step).astype(jnp.bfloat16)
        value[block] = jnp.where(low, 1.0, kv).astype(jnp.bfloat16)

    query_len[...] = jnp.zeros_like(query_len)
    key_len[...] = jnp.zeros_like(key_len)
    for t in range(HEADS):
        prepare(t)
        if not final:
            prepare_queries(t)
    if final:
        fetch.wait()
        for t in range(HEADS):
            prepare_queries(t)
    longest = longest_in[0] if final else jnp.max(query_len[...])
    fits = longest * jnp.max(key_len[...]) <= SAFE * SAFE
    if final:
        own_fits = longest >= 0.0
        fits = fits & own_fits
    else:
        longest_out[0] = jnp.where(fits, longest, -1.0)

    def block_at(block, count=1):
        return pl.ds(pl.multiple_of(block * rows, rows), count * rows)

    def scores(q, k):
        return lax.dot_general(q, k, (((1,), (1,)), ((), ())), preferred_element_type=jnp.float32)

    def weighted(p, v):
        return jnp.dot(p, v, preferred_element_type=jnp.float32)

    def finish(t):
        x = acc[t * rows : t * rows + half]
        y = acc[t * rows + half : (t + 1) * rows]
        low = low_lanes(x.shape)
        num = jnp.where(low, swap(x), y)
        den = jnp.where(low, x, swap(y))
        out_ref[t] = (num / den).astype(jnp.bfloat16)

    @pl.when(fits)
    def _():
        def spans(first, j):
            start, diagonal = first * per, j >= first
            if not diagonal:
                return [(0, start, 2 * per, j * per, per)]
            corner = j * per
            return [
                (0, corner, 1, corner, 1),
                (1, corner + 1, start + 2 * per - corner - 1, corner, per),
            ]

        def weights(p, first, j):
            version = int(j >= first)
            for at_row, row, count, column, width in spans(first, j):
                s = scores(query[block_at(row, count)], key[version, block_at(column, width)])
                here = slice(at_row * rows, (at_row + count) * rows)
                p[here, : width * rows] = jnp.exp2(s).astype(jnp.bfloat16)

        def gather(p, first, j):
            for at_row, row, count, column, width in spans(first, j):
                here = slice(at_row * rows, (at_row + count) * rows)
                v = value[block_at(column, width)]
                to = block_at(row, count)
                part = weighted(p[here, : width * rows], v)
                if j > 0:
                    acc[to] += part
                else:
                    acc[to] = state_in[to] + part if final else part

        todo = [(first, j) for first in range(0, tiles, 2) for j in range(first + 2)]
        slots = (p0, p1)
        weights(p0, *todo[0])
        for n, here in enumerate(todo):
            if n + 1 < len(todo):
                weights(slots[(n + 1) % 2], *todo[n + 1])
            gather(slots[n % 2], *here)
            if final and here[1] == here[0] + 1:
                for t in range(here[0] * per, (here[0] + 2) * per):
                    finish(t)

    @pl.when(jnp.logical_not(fits))
    def _():
        acc[...] = state_in[...] if final else jnp.zeros_like(acc)
        lane = lax.broadcasted_iota(jnp.int32, (TILE, LANES), 1)

        def spread(x, n):
            return jnp.max(jnp.where(lane == n, x, -jnp.inf), axis=-1, keepdims=True)

        def row_block(i, carry):
            to = at(i)
            if final:
                x = acc[to]
                top[...] = jnp.where(own_fits, 0.0, spread(x, HEAD // 2)) + jnp.zeros_like(x)
                acc[to] = jnp.where(lane < HEAD, spread(x, 0), x)
            else:
                top[...] = jnp.full_like(top, LOW)

            def key_block(j, carry):
                s = scores(query[to], key[(i == j).astype(jnp.int32), at(j)])
                old = top[...]
                new = jnp.maximum(old, jnp.max(s, axis=-1, keepdims=True))
                p = jnp.exp2(s - jnp.concatenate([new] * (TILE // LANES), axis=1))
                acc[to] = acc[to] * jnp.exp2(old - new) + weighted(p.astype(jnp.bfloat16), value[at(j)])
                top[...] = new
                return carry

            lax.fori_loop(0, i + 1, key_block, 0)
            if not final:
                x = acc[to]
                acc[to] = jnp.where((lane >= HEAD // 2) & (lane < HEAD), top[...], x)
            return carry

        lax.fori_loop(0, tiles, row_block, 0)
        if final:
            for t in range(HEADS):
                finish(t)


def attend(*operands):
    rows = operands[0].shape[1] * 2 // 3
    final = len(operands) > 1
    total = HEADS * rows
    whole = pl.BlockSpec(memory_space=pltpu.VMEM)
    scalar = pl.BlockSpec(memory_space=pltpu.SMEM)
    far = pl.BlockSpec(memory_space=pl.ANY)
    bf16_rows = pltpu.VMEM((total, LANES), jnp.bfloat16)
    f32_rows = pltpu.VMEM((total, LANES), jnp.float32)
    scratch = [
        pltpu.VMEM((HEADS, rows // 2, LANES), jnp.bfloat16),
        pltpu.SemaphoreType.DMA((1,)),
        f32_rows,
    ] * final + [
        pltpu.VMEM((TILE, LANES), jnp.float32),
        bf16_rows,
        pltpu.VMEM((2, total, LANES), jnp.bfloat16),
        bf16_rows,
        pltpu.VMEM((CHUNK, TILE), jnp.bfloat16),
        pltpu.VMEM((CHUNK, TILE), jnp.bfloat16),
        pltpu.VMEM((rows // 2, LANES), jnp.float32),
        pltpu.VMEM((rows, LANES), jnp.float32),
    ]
    if final:
        out = jax.ShapeDtypeStruct((HEADS, rows // 2, LANES), jnp.bfloat16)
    else:
        out = [
            jax.ShapeDtypeStruct((total, LANES), jnp.float32),
            jax.ShapeDtypeStruct((1,), jnp.float32),
        ]
    pairs = total * total // 2
    return pl.pallas_call(
        functools.partial(attend_kernel, final),
        in_specs=[far, whole, whole, scalar] if final else [whole],
        out_specs=whole if final else [whole, scalar],
        out_shape=out,
        scratch_shapes=scratch,
        compiler_params=pltpu.CompilerParams(vmem_limit_bytes=20 << 20),
        cost_estimate=pl.CostEstimate(
            flops=16 * pairs * LANES, bytes_accessed=8 << 20, transcendentals=pairs
        ),
        name="attend_other" if final else "attend_own",
    )(*operands)


def out_kernel(a_ref, w_ref, o_ref, flat):
    half = a_ref.shape[1]

    for p in range(HEADS // 2):
        a = a_ref[2 * p].astype(jnp.float32)
        b = a_ref[2 * p + 1].astype(jnp.float32)
        low = low_lanes(a.shape)
        cols = slice(p * LANES, (p + 1) * LANES)
        flat[:half, cols] = jnp.where(low, a, swap(b)).astype(jnp.bfloat16)
        flat[half:, cols] = jnp.where(low, swap(a), b).astype(jnp.bfloat16)
    for c in range(0, w_ref.shape[1], COLS):
        mixed = jnp.dot(flat[...], w_ref[:, c : c + COLS], preferred_element_type=jnp.float32)
        mixed = [mixed[step * half : (step + 1) * half] for step in range(2)]
        o_ref[:, :, c : c + COLS] = jnp.stack(mixed, axis=1).astype(jnp.bfloat16)


def project_out(att, w_out):
    half = att.shape[1]
    width = w_out.shape[0]
    rows = 2 * half
    return pl.pallas_call(
        out_kernel,
        in_specs=[pl.BlockSpec(memory_space=pltpu.VMEM)] * 2,
        out_specs=pl.BlockSpec(memory_space=pltpu.VMEM),
        out_shape=jax.ShapeDtypeStruct((half, 2, width), jnp.bfloat16),
        scratch_shapes=[pltpu.VMEM((rows, width), jnp.bfloat16)],
        compiler_params=pltpu.CompilerParams(vmem_limit_bytes=24 << 20),
        cost_estimate=pl.CostEstimate(
            flops=2 * rows * width * width, bytes_accessed=2 * width * width, transcendentals=0
        ),
        name="project_out",
    )(att, w_out)


def block_for(adjacency, mine):
    blocks = jnp.arange(adjacency.shape[0], dtype=jnp.int32)
    row = lax.dynamic_index_in_dim(adjacency, mine, 0, keepdims=False)
    others = row * (blocks != mine).astype(jnp.int32)
    return jnp.sum(others * blocks) + (1 - jnp.sum(others)) * mine


def choose(index, options):
    return functools.reduce(
        lambda rest, at: jnp.where(index == at, options[at], rest),
        range(len(options) - 1),
        options[-1],
    )


def same_core(x):
    count = lax.axis_size("var")
    held = []
    for offset in range(1, count // 2):
        pairs = [(v, (v + 2 * offset) % count) for v in range(count)]
        held.append(lax.ppermute(x, "var", pairs))
    return held


def pick_other(held, adjacency):
    count = lax.axis_size("var")
    chips = count // 2
    mine = lax.axis_index("var")
    want = block_for(adjacency, mine)
    partner_want = block_for(adjacency, mine ^ 1)
    away = lambda block: (mine // 2 - block // 2 + chips) % chips
    to_send = choose(away(partner_want), held)
    got = lax.ppermute(to_send, "var", [(v, v ^ 1) for v in range(count)])
    slot = jnp.where(want % 2 == mine % 2, away(want), chips)
    return choose(slot, held + [got])


def local(tokens, gain, w_query, w_key, w_value, w_out, adjacency):
    gain = gain.reshape(1, -1)
    held = same_core(tokens)
    packed = project(tokens, gain, (w_key, w_value, w_query))
    *held, _ = lax.optimization_barrier((*held, packed))
    x_other = pick_other([tokens, *held], adjacency)
    kv_other = project(x_other, gain, (w_key, w_value))
    packed, _ = lax.optimization_barrier((exchange(packed), kv_other))
    kv_other = exchange(kv_other)
    att = exchange(attend(packed, kv_other, *attend(packed)))
    return project_out(att, w_out)


def solution(mesh):
    in_specs = (P("var", "tm", None), P(), P(), P(), P(), P(), P())
    out_specs = P("var", "tm", None)
    return jax.shard_map(local, mesh=mesh, in_specs=in_specs, out_specs=out_specs, check_vma=False)
```

```python
import functools
import math

import jax
import jax.numpy as jnp
from jax import lax
from jax.experimental import pallas as pl
from jax.experimental.pallas import tpu as pltpu
from jax.sharding import PartitionSpec as P

HEADS = 16
HEAD = 64
LANES = 2 * HEAD
COLS = 512
CHUNK = 1024
TILE = 512
LOW = -1e30
SAFE = 80.0


def exchange(x):
    return lax.all_to_all(x, "tm", split_axis=0, concat_axis=0, tiled=True)


def low_lanes(shape):
    return lax.broadcasted_iota(jnp.int32, shape, len(shape) - 1) < HEAD


def swap(x):
    return pltpu.roll(x, HEAD, x.ndim - 1)


def normed_rows(x_ref, gain_ref):
    x = x_ref[...].astype(jnp.float32)
    x = jnp.concatenate([x[:, step] for step in range(x.shape[1])], axis=0)
    meansq = jnp.mean(x * x, axis=-1, keepdims=True)
    return (x * lax.rsqrt(meansq + 1e-06) * gain_ref[...]).astype(jnp.bfloat16)


def project_kernel(with_query, *refs):
    x_ref, gain_ref, wk_ref, wv_ref = refs[:4]
    out_ref, normed_ref = refs[-2:]
    step = pl.program_id(0)

    @pl.when(step == 0)
    def _():
        normed_ref[...] = normed_rows(x_ref, gain_ref)

    normed = normed_ref[...]
    rows = normed.shape[0]
    half = rows // 2
    k = jnp.dot(normed, wk_ref[...], preferred_element_type=jnp.float32)
    v = jnp.dot(normed, wv_ref[...], preferred_element_type=jnp.float32)
    if with_query:
        q = jnp.dot(normed, refs[4][...], preferred_element_type=jnp.float32)
        q = q * (math.log2(math.e) / HEAD**0.5)
    for p in range(COLS // LANES):
        cols = slice(p * LANES, (p + 1) * LANES)
        kt, vt = k[:, cols], v[:, cols]
        low = low_lanes(kt.shape)
        out_ref[2 * p, :rows] = jnp.where(low, kt, swap(vt)).astype(jnp.bfloat16)
        out_ref[2 * p + 1, :rows] = jnp.where(low, swap(kt), vt).astype(jnp.bfloat16)
        if with_query:
            top, bottom = q[:half, cols], q[half:, cols]
            low = low_lanes(top.shape)
            out_ref[2 * p, rows:] = jnp.where(low, top, swap(bottom)).astype(jnp.bfloat16)
            out_ref[2 * p + 1, rows:] = jnp.where(low, swap(top), bottom).astype(jnp.bfloat16)


def project(x, gain, weights):
    var_rows, step_rows, width = x.shape
    rows = var_rows * step_rows
    with_query = len(weights) == 3
    out_rows = rows + rows // 2 if with_query else rows
    flops = 2 * rows * width * width * len(weights)
    return pl.pallas_call(
        functools.partial(project_kernel, with_query),
        grid=(width // COLS,),
        in_specs=[
            pl.BlockSpec(x.shape, lambda j: (0, 0, 0)),
            pl.BlockSpec((1, width), lambda j: (0, 0)),
        ]
        + [pl.BlockSpec((width, COLS), lambda j: (0, j))] * len(weights),
        out_specs=pl.BlockSpec((COLS // HEAD, out_rows, LANES), lambda j: (j, 0, 0)),
        out_shape=jax.ShapeDtypeStruct((HEADS, out_rows, LANES), jnp.bfloat16),
        scratch_shapes=[pltpu.VMEM((rows, width), jnp.bfloat16)],
        compiler_params=pltpu.CompilerParams(vmem_limit_bytes=(56 if with_query else 20) << 20),
        cost_estimate=pl.CostEstimate(
            flops=flops, bytes_accessed=2 * width * width * len(weights) + 4 * rows * width,
            transcendentals=0,
        ),
        name="project_own" if with_query else "project_other",
    )(x, gain, *weights)


def other_kernel(x_ref, gain_ref, wk_ref, wv_ref, out_ref):
    normed = normed_rows(x_ref, gain_ref)
    for c in range(0, wk_ref.shape[1], COLS):
        cols = slice(c, c + COLS)
        k = jnp.dot(normed, wk_ref[:, cols], preferred_element_type=jnp.float32)
        v = jnp.dot(normed, wv_ref[:, cols], preferred_element_type=jnp.float32)
        for p in range(COLS // LANES):
            head = c // HEAD + 2 * p
            kt, vt = k[:, p * LANES : (p + 1) * LANES], v[:, p * LANES : (p + 1) * LANES]
            low = low_lanes(kt.shape)
            out_ref[head] = jnp.where(low, kt, swap(vt)).astype(jnp.bfloat16)
            out_ref[head + 1] = jnp.where(low, swap(kt), vt).astype(jnp.bfloat16)


def project_other(x, gain, weights):
    var_rows, step_rows, width = x.shape
    rows = var_rows * step_rows
    whole = pl.BlockSpec(memory_space=pltpu.VMEM)
    return pl.pallas_call(
        other_kernel,
        in_specs=[whole] * 4,
        out_specs=whole,
        out_shape=jax.ShapeDtypeStruct((HEADS, rows, LANES), jnp.bfloat16),
        compiler_params=pltpu.CompilerParams(vmem_limit_bytes=20 << 20),
        cost_estimate=pl.CostEstimate(
            flops=4 * rows * width * width,
            bytes_accessed=4 * width * width + 4 * rows * width,
            transcendentals=0,
        ),
        name="project_other",
    )(x, gain, *weights)


def attend_kernel(final, *refs):
    q_ref, *refs = refs
    kv_ref = q_ref
    if final:
        q_far = q_ref
        kv_ref, state_in, longest_in, out_ref, q_ref, sem, acc, *refs = refs
        fetch = pltpu.make_async_copy(q_far.at[:, kv_ref.shape[1] :], q_ref, sem.at[0])
        fetch.start()
    else:
        acc, longest_out, *refs = refs
    top, query, key, value, p0, p1, query_len, key_len = refs
    rows = kv_ref.shape[1] if final else q_ref.shape[1] * 2 // 3
    half = rows // 2
    per = TILE // rows
    tiles = HEADS // per
    lane_of = lambda axis: lax.broadcasted_iota(jnp.int32, (LANES, LANES), axis) // HEAD
    same_half = (lane_of(0) == lane_of(1)).astype(jnp.bfloat16)
    key_half = (lane_of(0) == 0).astype(jnp.bfloat16)

    def lengths(x, ones):
        return jnp.dot((x * x).astype(jnp.bfloat16), ones, preferred_element_type=jnp.float32)

    def at(tile, count=1):
        return pl.ds(pl.multiple_of(tile * TILE, TILE), count * TILE)

    def prepare_queries(t):
        x = q_ref[t, (0 if final else rows) :].astype(jnp.float32)
        if not final:
            query_len[...] = jnp.maximum(query_len[...], lengths(x, same_half))
        low = low_lanes(x.shape)
        lane = lax.broadcasted_iota(jnp.int32, x.shape, 1) - HEAD
        base = 2 * per * (t // per % 2)
        for part, y in enumerate((x, swap(x))):
            step = base + 2 * (t % per) + part
            later = jnp.where((lane > step) & (lane < base + 2 * per), LOW, jnp.float32(0.0))
            to = pl.ds(pl.multiple_of(t * rows + part * half, half), half)
            query[to] = jnp.where(low, y, later).astype(jnp.bfloat16)

    def prepare(t):
        block = pl.ds(pl.multiple_of(t * rows, rows), rows)
        kv = kv_ref[t, :rows].astype(jnp.float32)
        key_len[...] = jnp.maximum(key_len[...], lengths(kv, key_half))
        low = low_lanes(kv.shape)
        lane = lax.broadcasted_iota(jnp.int32, kv.shape, 1) - HEAD
        step = 2 * (t % (2 * per)) + lax.broadcasted_iota(jnp.int32, kv.shape, 0) // half
        is_step = jnp.where(lane == step, jnp.float32(1.0), jnp.float32(0.0))
        key[0, block] = jnp.where(low, kv, 0.0).astype(jnp.bfloat16)
        key[1, block] = jnp.where(low, kv, is_step).astype(jnp.bfloat16)
        value[block] = jnp.where(low, 1.0, kv).astype(jnp.bfloat16)

    query_len[...] = jnp.zeros_like(query_len)
    key_len[...] = jnp.zeros_like(key_len)
    for t in range(HEADS):
        prepare(t)
        if not final:
            prepare_queries(t)
    if final:
        fetch.wait()
        for t in range(HEADS):
            prepare_queries(t)
    longest = longest_in[0] if final else jnp.max(query_len[...])
    fits = longest * jnp.max(key_len[...]) <= SAFE * SAFE
    if final:
        own_fits = longest >= 0.0
        fits = fits & own_fits
    else:
        longest_out[0] = jnp.where(fits, longest, -1.0)

    def block_at(block, count=1):
        return pl.ds(pl.multiple_of(block * rows, rows), count * rows)

    def scores(q, k):
        return lax.dot_general(q, k, (((1,), (1,)), ((), ())), preferred_element_type=jnp.float32)

    def weighted(p, v):
        return jnp.dot(p, v, preferred_element_type=jnp.float32)

    def finish(t):
        x = acc[t * rows : t * rows + half]
        y = acc[t * rows + half : (t + 1) * rows]
        low = low_lanes(x.shape)
        num = jnp.where(low, swap(x), y)
        den = jnp.where(low, x, swap(y))
        out_ref[t] = (num / den).astype(jnp.bfloat16)

    @pl.when(fits)
    def _():
        def spans(first, j):
            start, diagonal = first * per, j >= first
            if not diagonal:
                return [(0, start, 2 * per, j * per, per)]
            corner = j * per
            return [
                (0, corner, 1, corner, 1),
                (1, corner + 1, start + 2 * per - corner - 1, corner, per),
            ]

        def weights(p, first, j):
            version = int(j >= first)
            for at_row, row, count, column, width in spans(first, j):
                s = scores(query[block_at(row, count)], key[version, block_at(column, width)])
                here = slice(at_row * rows, (at_row + count) * rows)
                p[here, : width * rows] = jnp.exp2(s).astype(jnp.bfloat16)

        def gather(p, first, j):
            for at_row, row, count, column, width in spans(first, j):
                here = slice(at_row * rows, (at_row + count) * rows)
                v = value[block_at(column, width)]
                to = block_at(row, count)
                part = weighted(p[here, : width * rows], v)
                if j > 0:
                    acc[to] += part
                else:
                    acc[to] = state_in[to] + part if final else part

        todo = [(first, j) for first in range(0, tiles, 2) for j in range(first + 2)]
        slots = (p0, p1)
        weights(p0, *todo[0])
        for n, here in enumerate(todo):
            if n + 1 < len(todo):
                weights(slots[(n + 1) % 2], *todo[n + 1])
            gather(slots[n % 2], *here)
            if final and here[1] == here[0] + 1:
                for t in range(here[0] * per, (here[0] + 2) * per):
                    finish(t)

    @pl.when(jnp.logical_not(fits))
    def _():
        acc[...] = state_in[...] if final else jnp.zeros_like(acc)
        lane = lax.broadcasted_iota(jnp.int32, (TILE, LANES), 1)

        def spread(x, n):
            return jnp.max(jnp.where(lane == n, x, -jnp.inf), axis=-1, keepdims=True)

        def row_block(i, carry):
            to = at(i)
            if final:
                x = acc[to]
                top[...] = jnp.where(own_fits, 0.0, spread(x, HEAD // 2)) + jnp.zeros_like(x)
                acc[to] = jnp.where(lane < HEAD, spread(x, 0), x)
            else:
                top[...] = jnp.full_like(top, LOW)

            def key_block(j, carry):
                s = scores(query[to], key[(i == j).astype(jnp.int32), at(j)])
                old = top[...]
                new = jnp.maximum(old, jnp.max(s, axis=-1, keepdims=True))
                p = jnp.exp2(s - jnp.concatenate([new] * (TILE // LANES), axis=1))
                acc[to] = acc[to] * jnp.exp2(old - new) + weighted(p.astype(jnp.bfloat16), value[at(j)])
                top[...] = new
                return carry

            lax.fori_loop(0, i + 1, key_block, 0)
            if not final:
                x = acc[to]
                acc[to] = jnp.where((lane >= HEAD // 2) & (lane < HEAD), top[...], x)
            return carry

        lax.fori_loop(0, tiles, row_block, 0)
        if final:
            for t in range(HEADS):
                finish(t)


def attend(*operands):
    rows = operands[0].shape[1] * 2 // 3
    final = len(operands) > 1
    total = HEADS * rows
    whole = pl.BlockSpec(memory_space=pltpu.VMEM)
    scalar = pl.BlockSpec(memory_space=pltpu.SMEM)
    far = pl.BlockSpec(memory_space=pl.ANY)
    bf16_rows = pltpu.VMEM((total, LANES), jnp.bfloat16)
    f32_rows = pltpu.VMEM((total, LANES), jnp.float32)
    scratch = [
        pltpu.VMEM((HEADS, rows // 2, LANES), jnp.bfloat16),
        pltpu.SemaphoreType.DMA((1,)),
        f32_rows,
    ] * final + [
        pltpu.VMEM((TILE, LANES), jnp.float32),
        bf16_rows,
        pltpu.VMEM((2, total, LANES), jnp.bfloat16),
        bf16_rows,
        pltpu.VMEM((CHUNK, TILE), jnp.bfloat16),
        pltpu.VMEM((CHUNK, TILE), jnp.bfloat16),
        pltpu.VMEM((rows // 2, LANES), jnp.float32),
        pltpu.VMEM((rows, LANES), jnp.float32),
    ]
    if final:
        out = jax.ShapeDtypeStruct((HEADS, rows // 2, LANES), jnp.bfloat16)
    else:
        out = [
            jax.ShapeDtypeStruct((total, LANES), jnp.float32),
            jax.ShapeDtypeStruct((1,), jnp.float32),
        ]
    pairs = total * total // 2
    return pl.pallas_call(
        functools.partial(attend_kernel, final),
        in_specs=[far, whole, whole, scalar] if final else [whole],
        out_specs=whole if final else [whole, scalar],
        out_shape=out,
        scratch_shapes=scratch,
        compiler_params=pltpu.CompilerParams(vmem_limit_bytes=20 << 20),
        cost_estimate=pl.CostEstimate(
            flops=16 * pairs * LANES, bytes_accessed=8 << 20, transcendentals=pairs
        ),
        name="attend_other" if final else "attend_own",
    )(*operands)


def out_kernel(a_ref, w_ref, o_ref, flat):
    half = a_ref.shape[1]

    for p in range(HEADS // 2):
        a = a_ref[2 * p].astype(jnp.float32)
        b = a_ref[2 * p + 1].astype(jnp.float32)
        low = low_lanes(a.shape)
        cols = slice(p * LANES, (p + 1) * LANES)
        flat[:half, cols] = jnp.where(low, a, swap(b)).astype(jnp.bfloat16)
        flat[half:, cols] = jnp.where(low, swap(a), b).astype(jnp.bfloat16)
    for c in range(0, w_ref.shape[1], COLS):
        mixed = jnp.dot(flat[...], w_ref[:, c : c + COLS], preferred_element_type=jnp.float32)
        mixed = [mixed[step * half : (step + 1) * half] for step in range(2)]
        o_ref[:, :, c : c + COLS] = jnp.stack(mixed, axis=1).astype(jnp.bfloat16)


def project_out(att, w_out):
    half = att.shape[1]
    width = w_out.shape[0]
    rows = 2 * half
    return pl.pallas_call(
        out_kernel,
        in_specs=[pl.BlockSpec(memory_space=pltpu.VMEM)] * 2,
        out_specs=pl.BlockSpec(memory_space=pltpu.VMEM),
        out_shape=jax.ShapeDtypeStruct((half, 2, width), jnp.bfloat16),
        scratch_shapes=[pltpu.VMEM((rows, width), jnp.bfloat16)],
        compiler_params=pltpu.CompilerParams(vmem_limit_bytes=24 << 20),
        cost_estimate=pl.CostEstimate(
            flops=2 * rows * width * width, bytes_accessed=2 * width * width, transcendentals=0
        ),
        name="project_out",
    )(att, w_out)


def block_for(adjacency, mine):
    blocks = jnp.arange(adjacency.shape[0], dtype=jnp.int32)
    row = lax.dynamic_index_in_dim(adjacency, mine, 0, keepdims=False)
    others = row * (blocks != mine).astype(jnp.int32)
    return jnp.sum(others * blocks) + (1 - jnp.sum(others)) * mine


def choose(index, options):
    return functools.reduce(
        lambda rest, at: jnp.where(index == at, options[at], rest),
        range(len(options) - 1),
        options[-1],
    )


def same_core(x):
    count = lax.axis_size("var")
    held = []
    for offset in range(1, count // 2):
        pairs = [(v, (v + 2 * offset) % count) for v in range(count)]
        held.append(lax.ppermute(x, "var", pairs))
    return held


def pick_other(held, adjacency):
    count = lax.axis_size("var")
    chips = count // 2
    mine = lax.axis_index("var")
    want = block_for(adjacency, mine)
    partner_want = block_for(adjacency, mine ^ 1)
    away = lambda block: (mine // 2 - block // 2 + chips) % chips
    to_send = choose(away(partner_want), held)
    got = lax.ppermute(to_send, "var", [(v, v ^ 1) for v in range(count)])
    slot = jnp.where(want % 2 == mine % 2, away(want), chips)
    return choose(slot, held + [got])


def local(tokens, gain, w_query, w_key, w_value, w_out, adjacency):
    gain = gain.reshape(1, -1)
    held = same_core(tokens)
    packed = project(tokens, gain, (w_key, w_value, w_query))
    *held, _ = lax.optimization_barrier((*held, packed))
    x_other = pick_other([tokens, *held], adjacency)
    kv_other = project_other(x_other, gain, (w_key, w_value))
    packed, _ = lax.optimization_barrier((exchange(packed), kv_other))
    kv_other = exchange(kv_other)
    att = exchange(attend(packed, kv_other, *attend(packed)))
    return project_out(att, w_out)


def solution(mesh):
    in_specs = (P("var", "tm", None), P(), P(), P(), P(), P(), P())
    out_specs = P("var", "tm", None)
    return jax.shard_map(local, mesh=mesh, in_specs=in_specs, out_specs=out_specs, check_vma=False)
```
